32 devices in a mesh: pole: 2 (over y), prow: 1, pcol: 16 (over z, x, core).
Axes of the slice: x: 2, y: 2, z: 4, core: 2. Of those that a mesh axis runs over, the one named last changes fastest.
Arguments:
- anc_inverse: float32 [12288, 6144], P(('pole', 'prow'), 'pcol'), parts along dimension 0, may hold values from -8 to 8
- anc_factor: float32 [12288, 768], P(('pole', 'pcol')), parts along dimension 0, may hold values from -0.078125 to 0.078125
- win_factor: float32 [1536, 768], P('pole'), parts along dimension 0, may hold values from -0.375 to 0.375
- pivot_inverse: float32 [6, 256, 256], P('pole'), parts along dimension 0, may hold values from -6 to 6
- structure: int32 [3, 24], replicated, may hold values 0 or 1
Outputs:
- anc_columns: float32 [12288, 768], P(('pole', 'prow', 'pcol')), parts along dimension 0
- win_inverse: float32 [1536, 768], P('pole'), parts along dimension 0
The draws below stay inside these ranges and needn't reach their ends.
There are 2 independent parts, one for each index of `pole`. The reference program is written for one: setup_inputs(seed, part) draws one part's arguments, and reference() takes and returns one part's arrays. A program takes and returns all parts, laid end to end along the dimension named above; an argument that names none is the same for every part. Nothing has to cross between parts.
All inputs are finite; a program needn't handle non-finite values.
Results may differ from the reference program's by a relative error of at most 0.0001.
Values sent between devices are 32-bit elements; how exact they have to be, the bound alone decides.
A program may use at most 128 MiB of HBM per device.

```python
import jax
import jax.numpy as jnp
from jax import lax

W = 256
STEPS = 3
NA = 6144
NAB = 24
SW = 768


def draw_anc_inverse(key, part):
    entry_key = jax.random.fold_in(jax.random.fold_in(key, 11), 0)
    entries = jnp.clip(jax.random.normal(entry_key, (NA, NA), jnp.float32), -5.0, 5.0)
    return (entries + entries.T) * 0.7071


def plant(values, key, low, high):
    index_at = [jax.random.randint(jax.random.fold_in(key, axis), (), 0, length) for axis, length in enumerate(values.shape)]
    widest = values.shape.index(max(values.shape))
    next_to = index_at[:widest] + [(index_at[widest] + 1) % values.shape[widest]] + index_at[widest + 1:]
    return values.at[tuple(index_at)].set(low).at[tuple(next_to)].set(high)


def steps_of(stream_key, dims, cuts, least, high):
    gain = 1.0
    for axis_at, shards_of in cuts:
        heights = jax.random.uniform(jax.random.fold_in(jax.random.fold_in(stream_key, 6), axis_at), (shards_of,), jnp.float32, least / len(cuts), high / len(cuts))
        gain = gain * jnp.repeat(jnp.exp(heights), dims[axis_at] // shards_of).reshape((-1,) + (1,) * (len(dims) - 1 - axis_at))
    return gain


def scatter_about(rng, shape, deviation, reach, cuts=(), kind=jnp.bfloat16):
    array = deviation * jax.random.normal(rng, shape, jnp.float32)
    if cuts:
        array = array * steps_of(rng, shape, cuts, -0.22, 0.18)
    return jnp.clip(array, -reach, reach).astype(kind)


def setup_inputs(seed: int = 0, part: int = 0) -> dict:
    arg_keys = jax.random.split(jax.random.key(seed), 6)
    part_keys = jax.random.split(jax.random.fold_in(arg_keys[5], part), 6)
    anc_inverse = draw_anc_inverse(jax.random.fold_in(jax.random.fold_in(arg_keys[5], part), 71), part)
    anc_factor = scatter_about(part_keys[1], (NA, SW), NA ** -0.5, 0.078125, ((0, 16),), jnp.float32)
    win_factor = scatter_about(part_keys[2], (SW, SW), W ** -0.5, 0.375, (), jnp.float32)
    pivot_inverse = scatter_about(part_keys[3], (STEPS, W, W), 1.0, 6.0, (), jnp.float32)
    structure = plant((jax.random.randint(arg_keys[4], (STEPS, NAB), 0, 4) < 3).astype(jnp.int32), jax.random.fold_in(arg_keys[4], 1), 0, 1)
    return dict(anc_inverse=anc_inverse, anc_factor=anc_factor, win_factor=win_factor, pivot_inverse=pivot_inverse, structure=structure)


precise = lax.Precision.HIGHEST


def product(left, right):
    return jnp.dot(left, right, precision=precise, preferred_element_type=jnp.float32)


def reference(anc_inverse, anc_factor, win_factor, pivot_inverse, structure):
    row_block = (jnp.arange(NA) // W).astype(jnp.int32)
    kept_rows = jnp.take(structure, row_block, axis=1).astype(jnp.float32).T
    column_store = {}
    window_blocks = {}
    for k in range(STEPS - 1, -1, -1):
        first_col = k * W
        factor_now = anc_factor[:, first_col:first_col + W] * kept_rows[:, k:k + 1]
        product_term = product(anc_inverse, factor_now)
        finished = list(range(k + 1, STEPS))
        if finished:
            stacked = jnp.concatenate([column_store[j] for j in finished], axis=1)
            column_now = -(product_term + product(stacked, win_factor[first_col + W:, first_col:first_col + W]))
        else:
            column_now = -product_term
        for j in finished:
            running = product(column_store[j].T, factor_now)
            for i in finished:
                running = running + product(window_blocks[(j, i)], win_factor[i * W:(i + 1) * W, first_col:first_col + W])
            window_blocks[(j, k)] = -running
            window_blocks[(k, j)] = -running.T
        pivot_block = pivot_inverse[k] - product(factor_now.T, column_now)
        for j in finished:
            pivot_block = pivot_block - product(win_factor[j * W:(j + 1) * W, first_col:first_col + W].T, window_blocks[(j, k)])
        window_blocks[(k, k)] = pivot_block
        column_store[k] = column_now
    anc_columns = jnp.concatenate([column_store[k] for k in range(STEPS)], axis=1)
    win_inverse = jnp.concatenate([jnp.concatenate([window_blocks[(i, k)] for k in range(STEPS)], axis=1) for i in range(STEPS)], axis=0)
    return (anc_columns, win_inverse)
```

```python
import functools

import jax
import jax.numpy as jnp
from jax import lax
from jax.experimental import pallas as pl
from jax.experimental.pallas import tpu as pltpu
from jax.sharding import PartitionSpec as P

MESH = pl.DeviceIdType.MESH
UP, DOWN, ACROSS, MATE = range(4)
Z = 4
LANES = 8


def split(value):
    high = value.astype(jnp.bfloat16)
    low = (value - high.astype(jnp.float32)).astype(jnp.bfloat16)
    return high, low


def dot3(left, right):
    (lh, ll), (rh, rl) = left, right
    dot = functools.partial(jnp.dot, preferred_element_type=jnp.float32)
    return dot(lh, rh) + (dot(lh, rl) + dot(ll, rh))


def mul(left, right):
    return dot3(split(left), split(right))


STAGES = 2
SLOTS = 8


def item_list(u):
    if u == 0:
        rest = [("R1", 3), ("R0", 3), ("R1", 2), ("R0", 2), ("R1", 1), ("R0", 1)]
        return [("G", 0), ("H", 0)] + rest
    if u == 1:
        rest = [("R1", 3), ("R0", 3), ("R1", 2), ("R0", 2)]
        return [("G", 1), ("H", 1), ("G", 0), ("H", 0)] + rest
    rest = [("G", 1), ("H", 1), ("G", 0), ("H", 0), ("R1", 3), ("R0", 3)]
    return [("G", 2), ("H", 2)] + rest


def order_static(z):
    return ([0, 1, 2, 3], [1, 0, 2, 3], [2, 3, 1, 0], [3, 2, 1, 0])[z]


def fused_kernel(names, width, anc_ref, fac_ref, win_ref, piv_ref, str_ref, cols_ref, out_ref, *scratch):
    m = dict(zip(names, scratch, strict=True))
    fac, a_buf, win_st, piv_st = m["fac"], m["a_buf"], m["win"], m["piv"]
    lr_hi, lr_lo, lt_hi, lt_lo = m["lr_hi"], m["lr_lo"], m["lt_hi"], m["lt_lo"]
    tr_hi, tr_lo = m["tr_hi"], m["tr_lo"]
    own, near, y_own, y_near = m["own"], m["near"], m["y_own"], m["y_near"]
    p0, m0i, x0i, z0i = m["p0"], m["m0i"], m["x0i"], m["z0i"]
    p1, m1i, x1i, z1i = m["p1"], m["m1i"], m["x1i"], m["z1i"]

    me = lax.axis_index("pcol")
    core = lax.rem(me, 2)
    x = lax.rem(me // 2, 2)
    z = me // 4
    lane = me // 2
    rows = fac.shape[0]
    tile = width // 2
    mate = me + 1 - 2 * core

    def index(zz, xx, cc):
        return (zz * 2 + xx) * 2 + cc

    x_other = 1 - x
    across = index(z, x_other, core)

    def order(t):
        inner = (0, 0, 2, 3) if t else (1, 1, 1, 1)
        lowmid = inner[t] if t else 1
        highmid = 3 - lowmid
        return jnp.where(z == 0, t, jnp.where(z == 1, lowmid, jnp.where(z == 2, highmid, 3 - t)))

    def job_chip(q):
        return order(3 - q // 2) * 2 + (1 - x if q % 2 == 0 else x)

    def load_anc(q):
        at = pl.ds(pl.multiple_of(job_chip(q) * 2 * rows, 2 * rows), 2 * rows)
        return pltpu.make_async_copy(anc_ref.at[at, :], a_buf.at[q % 4], m["load_sem"].at[q])

    load_fac = pltpu.make_async_copy(fac_ref, fac, m["load_sem"].at[8])
    load_piv = pltpu.make_async_copy(piv_ref, piv_st, m["load_sem"].at[9])
    win_pairs = [(2, 1), (1, 0), (2, 0)]

    def load_win(n):
        j, k = win_pairs[n]
        block = win_ref.at[pl.ds(j * width, width), pl.ds(k * width, width)]
        return pltpu.make_async_copy(block, win_st.at[n], m["load_sem"].at[10 + n])

    load_fac.start()
    for q in range(4):
        load_anc(q).start()

    barrier = pltpu.get_barrier_semaphore()
    for d in range(1, LANES):
        peer = lax.rem(lane + d, LANES) * 2 + core
        pl.semaphore_signal(barrier, inc=1, device_id={"pcol": peer}, device_id_type=MESH)
    pl.semaphore_signal(barrier, inc=1, device_id={"pcol": mate}, device_id_type=MESH)

    common = []
    by_z = [[] for _ in range(Z)]
    log = [common]

    def go(make):
        make().start()
        log[0].append(make)

    def remote(src, dst, ssem, rsem, dest):
        return pltpu.make_async_remote_copy(
            src_ref=src, dst_ref=dst, send_sem=ssem, recv_sem=rsem, device_id={"pcol": dest}, device_id_type=MESH
        )

    def arrive(dst, rsem):
        remote(dst, dst, rsem, rsem, mate).wait_recv()

    def core_rows(c):
        return pl.ds(pl.multiple_of(c * rows, rows), rows)

    def own_at(s, zz, xx, c):
        return own.at[s, zz * 2 + xx, core_rows(c), :]

    def near_at(s, zz, c):
        return near.at[s, zz, core_rows(c), :]

    def own_send(s, zz, xx, kind, dest):
        def make():
            ref = own_at(s, zz, xx, core)
            return remote(ref, ref, m["own_s"].at[s, kind, zz * 2 + xx], m["own_r"].at[s, zz * 2 + xx, core], dest)
        go(make)

    def near_send(s, zz, kind, dest):
        def make():
            ref = near_at(s, zz, core)
            return remote(ref, ref, m["near_s"].at[s, kind, zz], m["near_r"].at[s, zz, core], dest)
        go(make)

    def own_wait(s, zz, xx, c):
        arrive(own_at(s, zz, xx, c), m["own_r"].at[s, zz * 2 + xx, c])

    def near_wait(s, zz, c):
        arrive(near_at(s, zz, c), m["near_r"].at[s, zz, c])

    def columns(t):
        return slice(t * tile, (t + 1) * tile)

    def mask(t):
        for piece in range(rows // tile):
            block = (me * (rows // tile) + piece) // 2
            kept = str_ref[t // 2, block].astype(jnp.float32)
            at = slice(piece * tile, (piece + 1) * tile)
            fac[at, columns(t)] = fac[at, columns(t)] * kept

    own_tiles, near_tiles, sum_tiles = (5, 2), (4, 1), (3, 0)

    load_fac.wait()
    mask(own_tiles[0])
    own[0, lane, core_rows(core), :] = fac[:, columns(own_tiles[0])]
    pl.semaphore_wait(barrier, LANES)

    def in_direction(direction, zz):
        return zz if direction == UP else Z - 1 - zz

    z_dests = (me + 4, me - 4)

    def z_dest(direction):
        return z_dests[direction]

    def landing(direction, zz, dest_z):
        return Z if direction == DOWN and dest_z == zz else dest_z

    def z_send(direction, zz, n):
        s, (kind, v) = n // SLOTS, item_list(in_direction(direction, zz))[n % SLOTS]
        vz = in_direction(direction, v)
        first = in_direction(direction, zz) == 0
        dest = z_dest(direction)
        there = zz + 1 if direction == UP else zz - 1
        if kind == "G":
            own_send(s, vz, x, direction, dest)
        elif kind == "H":
            near_send(s, vz, direction, dest)
        elif kind == "R1":
            arrive(m1i.at[s, vz], m["m1_r"].at[s, vz])
            value = p1[s, 0, vz] + m1i[s, vz]
            if not first:
                value = value + z1i[s, vz]
            p1[s, 0, vz] = value
            at = landing(direction, there, vz)
            go(lambda: remote(p1.at[s, 0, vz], z1i.at[s, at], m["z1_s"].at[s, vz], m["z1_r"].at[s, at], z_dest(direction)))
        else:
            arrive(m0i.at[s, 0, vz], m["m0_r"].at[s, 0, vz])
            arrive(x0i.at[s, vz], m["x0_r"].at[s, vz])
            value = p0[s, 0, 0, vz] + m0i[s, 0, vz] + x0i[s, vz]
            if not first:
                value = value + z0i[s, vz]
            p0[s, 0, 0, vz] = value
            at = landing(direction, there, vz)
            go(lambda: remote(p0.at[s, 0, 0, vz], z0i.at[s, at], m["z0_s"].at[s, vz], m["z0_r"].at[s, at], z_dest(direction)))

    def z_arrival(direction, zz, n):
        u = in_direction(direction, zz)
        s, (kind, v) = n // SLOTS, item_list(u - 1)[n % SLOTS]
        vz = in_direction(direction, v)
        if kind == "G":
            own_wait(s, vz, x, core)
            own_send(s, vz, x, MATE, mate)
        elif kind == "H":
            near_wait(s, vz, core)
            near_send(s, vz, MATE - 1, mate)
        elif kind == "R1":
            at = landing(direction, zz, vz)
            arrive(z1i.at[s, at], m["z1_r"].at[s, at])
        else:
            at = landing(direction, zz, vz)
            arrive(z0i.at[s, at], m["z0_r"].at[s, at])

    def x_sum(s, v):
        arrive(m0i.at[s, 1, v], m["m0_r"].at[s, 1, v])
        p0[s, 0, 1, v] = p0[s, 0, 1, v] + m0i[s, 1, v]
        go(lambda: remote(p0.at[s, 0, 1, v], x0i.at[s, v], m["x0_s"].at[s, v], m["x0_r"].at[s, v], across))

    def x_near(s, zz):
        arrive(m1i.at[s, zz], m["m1_r"].at[s, zz])
        value = p1[s, 0, zz] + m1i[s, zz]
        if zz > 0:
            value = value + z1i[s, zz]
        if zz < Z - 1:
            value = value + z1i[s, Z]
        p1[s, 0, zz] = value
        go(lambda: remote(p1.at[s, 0, zz], x1i.at[s], m["x1_s"].at[s], m["x1_r"].at[s], across))

    def x_step(s, n, zz):
        near_first = order_static(zz)
        if n in (1, 3, 5):
            own_send(s, near_first[(n + 1) // 2], x, ACROSS, across)
        elif n in (2, 4, 6):
            x_sum(s, near_first[3 - n // 2])
        else:
            x_near(s, zz)

    def x_arrival(s, t, zz):
        v = order_static(zz)[t]
        own_wait(s, v, x_other, core)
        own_send(s, v, x_other, MATE, mate)

    def events(step):
        for zz in range(Z):
            log[0] = by_z[zz]

            @pl.when(z == zz)
            def _():
                for direction in (UP, DOWN):
                    if in_direction(direction, zz) > 0 and 0 <= step - 1 < STAGES * SLOTS:
                        z_arrival(direction, zz, step - 1)
                for direction in (UP, DOWN):
                    if in_direction(direction, zz) < Z - 1 and 2 <= step + 1 < STAGES * SLOTS:
                        z_send(direction, zz, step + 1)
                for s in range(STAGES):
                    n = step - SLOTS * s
                    if 1 <= n <= 7:
                        x_step(s, n, zz)
                    if n in (2, 3, 5, 7):
                        x_arrival(s, (0, 0, 0, 1, 0, 2, 0, 3)[n] if n > 2 else 0, zz)

            log[0] = common

    def begin(s):
        own_send(s, z, x, ACROSS, across)
        own_send(s, z, x, MATE, mate)
        near_send(s, z, MATE - 1, mate)

    for zz in range(Z):
        log[0] = by_z[zz]

        @pl.when(z == zz)
        def _():
            for direction in (UP, DOWN):
                if in_direction(direction, zz) < Z - 1:
                    z_send(direction, zz, 0)

        log[0] = common
    own_send(0, z, x, ACROSS, across)
    own_send(0, z, x, MATE, mate)

    mask(near_tiles[0])
    near[0, z, core_rows(core), :] = fac[:, columns(near_tiles[0])]
    near_send(0, z, MATE - 1, mate)
    for zz in range(Z):
        log[0] = by_z[zz]

        @pl.when(z == zz)
        def _():
            for direction in (UP, DOWN):
                if in_direction(direction, zz) < Z - 1:
                    z_send(direction, zz, 1)

        log[0] = common

    for t in (sum_tiles[0], sum_tiles[1], near_tiles[1], own_tiles[1]):
        mask(t)
    for n, t in enumerate((sum_tiles[0], sum_tiles[1], near_tiles[0], near_tiles[1])):
        high, low = split(fac[:, columns(t)])
        lr_hi[:, columns(n)] = high
        lr_lo[:, columns(n)] = low

    def chip_job(q):
        v = order(3 - q // 2)
        other = q % 2 == 0
        side = 1 if other else 0
        chip = job_chip(q)
        load_anc(q).wait()

        def both(i, carry):
            c = core + (1 - 2 * core) * (1 - i)
            pair = split(a_buf[q % 4, core_rows(c), :])
            count = (4 if other else 2) * tile
            value = dot3(pair, (lr_hi[:, :count], lr_lo[:, :count]))
            for s in range(STAGES):
                p0[s, 1 - i, side, v] = value[:, columns(s)]
                if other:
                    p1[s, 1 - i, v] = value[:, columns(2 + s)]
            return carry

        lax.fori_loop(0, 2, both, 0)
        for s in range(STAGES):
            go(lambda s=s: remote(p0.at[s, 1, side, v], m0i.at[s, side, v], m["m0_s"].at[s, side, v], m["m0_r"].at[s, side, v], mate))
            if other:
                go(lambda s=s: remote(p1.at[s, 1, v], m1i.at[s, v], m["m1_s"].at[s, v], m["m1_r"].at[s, v], mate))

        def flip(c, carry):
            high, low = split(a_buf[q % 4, core_rows(c), :].T)
            at = pl.ds(pl.multiple_of(c * rows, rows), rows)
            tr_hi[chip, :, at] = high
            tr_lo[chip, :, at] = low
            return carry

        lax.fori_loop(0, 2, flip, 0)
        if q + 4 < 8:
            load_anc(q + 4).start()

    def pair_job(block, total, chip, first):
        high, low = split(block)
        left, rest = tr_hi[chip], tr_lo[chip]
        wide = jnp.dot(left, jnp.concatenate([high, low], axis=1), preferred_element_type=jnp.float32)
        value = wide[:, :tile] + (wide[:, tile:] + jnp.dot(rest, high, preferred_element_type=jnp.float32))
        if first:
            total[...] = value
        else:
            total[...] += value

    def own_job(s, t, other):
        zz = order(t)
        xx = 1 - x if other else x
        own_wait(s, zz, xx, 1 - core)
        pair_job(own[s, zz * 2 + xx], y_own.at[s], zz * 2 + xx, t == 0 and not other)

    def near_job(s, t):
        zz = order(t)
        near_wait(s, zz, 1 - core)
        pair_job(near[s, zz], y_near.at[s], zz * 2 + x, t == 0)

    def finish(s):
        cols_ref[:, columns(own_tiles[s])] = y_own[s]
        arrive(x1i.at[s], m["x1_r"].at[s])
        cols_ref[:, columns(near_tiles[s])] = y_near[s] + x1i[s]
        arrive(m0i.at[s, 0, z], m["m0_r"].at[s, 0, z])
        arrive(x0i.at[s, z], m["x0_r"].at[s, z])
        value = p0[s, 0, 0, z] + m0i[s, 0, z] + x0i[s, z]
        low = z0i[s, z]
        high = z0i[s, Z]
        value = value + jnp.where(z > 0, low, 0.0) + jnp.where(z < Z - 1, high, 0.0)
        cols_ref[:, columns(sum_tiles[s])] = value

    half_cols = 3 * tile
    sum_list = (
        [(q, p) for q in (3, 4, 5) for p in range(q + 1)],
        [(q, p) for q in (0, 1, 2) for p in range(q + 1)],
    )

    def inner_early():
        flipped = split(cols_ref[:, half_cols:].T)
        value = dot3(flipped, split(fac[...]))
        for n, (q, p) in enumerate(sum_list[0]):
            m["part0"][n] = value[(q - 3) * tile : (q - 2) * tile, columns(p)]

    def inner_late():
        value = dot3((lt_hi[...], lt_lo[...]), split(cols_ref[:, :half_cols]))
        for n, (q, p) in enumerate(sum_list[1]):
            m["part1"][n] = value[columns(q), columns(p)]

    groups = {
        "mate": (2, core, lambda n: index(z, x, n)),
        "x": (2, x, lambda n: index(z, n, core)),
        "z": (Z, z, lambda n: index(n, x, core)),
        "lane": (LANES, lane, lambda n: n * 2 + core),
    }

    def reducer(s):
        plan = LEVELS[s]
        sums = m[f"sum{s}"]
        sizes = [tile]
        for name in plan:
            sizes.append(sizes[-1] // groups[name][0])
        base = [0]
        for name, size in zip(plan, sizes[1:]):
            base.append(base[-1] + groups[name][1] * size)

        def held(level):
            return m[f"part{s}"] if level == 0 else m[f"held{s}_{level}"]

        def peer_of(level, d):
            count, mine, _ = groups[plan[level]]
            return 1 - mine if count == 2 else lax.rem(mine + d, count)

        def send_down(level):
            count, mine, device = groups[plan[level]]
            size = sizes[level + 1]
            for d in range(1, count):
                def make(d=d):
                    peer = peer_of(level, d)
                    src = held(level).at[:, pl.ds(pl.multiple_of(peer * size, size), size), :]
                    return remote(
                        src, m[f"slot{s}_{level}"].at[mine], m[f"ds{s}"].at[level, peer], m[f"dr{s}"].at[level, mine], device(peer)
                    )
                go(make)

        def take_down(level):
            count, mine, device = groups[plan[level]]
            size = sizes[level + 1]
            slot = m[f"slot{s}_{level}"]
            total = held(level)[:, pl.ds(pl.multiple_of(mine * size, size), size), :]
            for d in range(1, count):
                peer = peer_of(level, d)
                arrive(slot.at[peer], m[f"dr{s}"].at[level, peer])
                total = total + slot[peer]
            if level + 1 < len(plan):
                held(level + 1)[...] = total
            else:
                sums[:, pl.ds(pl.multiple_of(base[-1], size), size), :] = total

        def part_at(level, owner):
            size = sizes[level + 1]
            return sums.at[:, pl.ds(pl.multiple_of(base[level] + owner * size, size), size), :]

        def send_up(level):
            count, mine, device = groups[plan[level]]
            for d in range(1, count):
                def make(d=d):
                    peer = peer_of(level, d)
                    ref = part_at(level, mine)
                    return remote(ref, ref, m[f"us{s}"].at[level, peer], m[f"ur{s}"].at[level, mine], device(peer))
                go(make)

        def take_up(level):
            count, mine, device = groups[plan[level]]
            for d in range(1, count):
                peer = peer_of(level, d)
                arrive(part_at(level, peer), m[f"ur{s}"].at[level, peer])

        steps = [lambda: send_down(0)]
        for level in range(len(plan)):
            def step(level=level):
                take_down(level)
                if level + 1 < len(plan):
                    send_down(level + 1)
                else:
                    send_up(level)
            steps.append(step)
        for level in range(len(plan) - 1, -1, -1):
            def step(level=level):
                take_up(level)
                if level > 0:
                    send_up(level - 1)
            steps.append(step)
        return steps

    inner = m["inner"]
    blocks = [(2, 2), (2, 1), (2, 0), (1, 1), (1, 0), (0, 0)]

    def place(s):
        for n, (q, p) in enumerate(sum_list[s]):
            value = m[f"sum{s}"][n]
            at = blocks.index((q // 2, p // 2))
            inner[at, (q % 2) * tile : (q % 2 + 1) * tile, (p % 2) * tile : (p % 2 + 1) * tile] = value
            if q // 2 == p // 2 and q != p:
                inner[at, (p % 2) * tile : (p % 2 + 1) * tile, (q % 2) * tile : (q % 2 + 1) * tile] = value.T

    def n_block(j, k):
        return inner[blocks.index((j, k))]

    def fac_block(j, k):
        return win_st[win_pairs.index((j, k))]

    def put(j, k, value):
        out_ref[j * width : (j + 1) * width, k * width : (k + 1) * width] = value

    def got(j, k):
        return out_ref[j * width : (j + 1) * width, k * width : (k + 1) * width]

    early = m["early"]

    def window_first():
        put(2, 2, piv_st[2] + n_block(2, 2))
        value = n_block(2, 1) - mul(got(2, 2), fac_block(2, 1))
        put(2, 1, value)
        put(1, 2, value.T)
        value = n_block(2, 0) - mul(got(2, 1), fac_block(1, 0)) - mul(got(2, 2), fac_block(2, 0))
        put(2, 0, value)
        put(0, 2, value.T)

    def window_second():
        flip21 = split(fac_block(2, 1).T)
        known = piv_st[1] - mul(n_block(2, 1).T, fac_block(2, 1)) - dot3(flip21, split(got(2, 1)))
        early[0] = known
        turned = dot3(flip21, split(n_block(2, 0)))
        left = jnp.concatenate([fac_block(2, 1).T, known, got(1, 2)], axis=1)
        right = jnp.concatenate([n_block(2, 0), fac_block(1, 0), fac_block(2, 0)], axis=0)
        early[1] = mul(left, right)
        early[2] = (
            piv_st[0]
            + mul(turned.T, fac_block(1, 0))
            - mul(n_block(2, 0).T, fac_block(2, 0))
            - mul(fac_block(2, 0).T, got(2, 0))
        )

    def window_last():
        put(1, 1, early[0] + n_block(1, 1))
        value = n_block(1, 0) - early[1] - mul(n_block(1, 1), fac_block(1, 0))
        put(1, 0, value)
        put(0, 1, value.T)
        put(0, 0, early[2] + n_block(0, 0) - mul(n_block(1, 0).T, fac_block(1, 0)) - mul(fac_block(1, 0).T, value))

    def column(k):
        return cols_ref[:, k * width : (k + 1) * width]

    def put_column(k):
        value = column(k)
        for j in range(k + 1, 3):
            value = value + mul(column(j), fac_block(j, k))
        cols_ref[:, k * width : (k + 1) * width] = -value

    chip_job(0)
    chip_job(1)
    x_sum(0, order(3))
    load_piv.start()
    for n in range(3):
        load_win(n).start()
    events(1)
    chip_job(2)
    chip_job(3)
    events(2)
    chip_job(4)
    chip_job(5)
    events(3)
    chip_job(6)
    chip_job(7)
    events(4)
    own[1, lane, core_rows(core), :] = fac[:, columns(own_tiles[1])]
    near[1, z, core_rows(core), :] = fac[:, columns(near_tiles[1])]
    own_job(0, 0, False)
    own_job(0, 1, False)
    events(5)
    near_job(0, 0)
    near_job(0, 1)
    own_job(0, 0, True)
    own_job(0, 1, True)
    events(6)
    own_job(0, 2, False)
    near_job(0, 2)
    own_job(0, 2, True)
    events(7)
    begin(1)
    x_sum(1, order(3))
    own_job(0, 3, False)
    high, low = split(fac[:, :half_cols].T)
    lt_hi[...] = high
    lt_lo[...] = low
    events(8)
    near_job(0, 3)
    own_job(0, 3, True)
    events(9)
    finish(0)
    inner_early()
    cols_ref[:, 2 * width :] = -cols_ref[:, 2 * width :]
    first, last = reducer(0), reducer(1)
    first[0]()
    events(10)
    first[1]()
    own_job(1, 0, False)
    own_job(1, 1, False)
    events(11)
    first[2]()
    near_job(1, 0)
    near_job(1, 1)
    own_job(1, 0, True)
    events(12)
    first[3]()
    own_job(1, 1, True)
    events(13)
    first[4]()
    own_job(1, 2, False)
    near_job(1, 2)
    events(14)
    first[5]()
    own_job(1, 2, True)
    load_piv.wait()
    for n in range(3):
        load_win(n).wait()
    events(15)
    first[6]()
    own_job(1, 3, False)
    place(0)
    window_first()
    near_job(1, 3)
    events(16)
    own_job(1, 3, True)
    finish(1)
    inner_late()
    last[0]()
    window_second()
    last[1]()
    put_column(1)
    last[2]()
    put_column(0)
    for step in last[3:]:
        step()
    place(1)
    window_last()

    for make in common:
        make().wait_send()
    for zz in range(Z):

        @pl.when(z == zz)
        def _():
            for make in by_z[zz]:
                make().wait_send()


LEVELS = (("mate", "x", "z"), ("mate", "lane"))
COUNT = dict(mate=2, x=2, z=Z, lane=LANES)


def fused(anc_inverse, anc_factor, win_factor, pivot_inverse, structure):
    steps, width = pivot_inverse.shape[:2]
    rows, all_cols = anc_factor.shape
    tile = width // 2
    f32, b16 = jnp.float32, jnp.bfloat16
    dma = pltpu.SemaphoreType.DMA
    block = (rows, tile)
    pair = (2 * rows, tile)
    spaces = dict(
        fac=pltpu.VMEM((rows, all_cols), f32),
        a_buf=pltpu.VMEM((4, 2 * rows, rows), f32),
        win=pltpu.VMEM((3, width, width), f32),
        piv=pltpu.VMEM(pivot_inverse.shape, f32),
        lr_hi=pltpu.VMEM((rows, 4 * tile), b16),
        lr_lo=pltpu.VMEM((rows, 4 * tile), b16),
        lt_hi=pltpu.VMEM((3 * tile, rows), b16),
        lt_lo=pltpu.VMEM((3 * tile, rows), b16),
        tr_hi=pltpu.VMEM((LANES, rows, 2 * rows), b16),
        tr_lo=pltpu.VMEM((LANES, rows, 2 * rows), b16),
        own=pltpu.VMEM((STAGES, LANES, *pair), f32),
        near=pltpu.VMEM((STAGES, Z, *pair), f32),
        y_own=pltpu.VMEM((STAGES, *block), f32),
        y_near=pltpu.VMEM((STAGES, *block), f32),
        p0=pltpu.VMEM((STAGES, 2, 2, Z, *block), f32),
        m0i=pltpu.VMEM((STAGES, 2, Z, *block), f32),
        x0i=pltpu.VMEM((STAGES, Z, *block), f32),
        z0i=pltpu.VMEM((STAGES, Z + 1, *block), f32),
        p1=pltpu.VMEM((STAGES, 2, Z, *block), f32),
        m1i=pltpu.VMEM((STAGES, Z, *block), f32),
        x1i=pltpu.VMEM((STAGES, *block), f32),
        z1i=pltpu.VMEM((STAGES, Z + 1, *block), f32),
        inner=pltpu.VMEM((6, width, width), f32),
        early=pltpu.VMEM((3, width, width), f32),
        load_sem=dma((13,)),
        own_s=dma((STAGES, 4, LANES)),
        own_r=dma((STAGES, LANES, 2)),
        near_s=dma((STAGES, 3, Z)),
        near_r=dma((STAGES, Z, 2)),
        m0_s=dma((STAGES, 2, Z)),
        m0_r=dma((STAGES, 2, Z)),
        x0_s=dma((STAGES, Z)),
        x0_r=dma((STAGES, Z)),
        z0_s=dma((STAGES, Z)),
        z0_r=dma((STAGES, Z + 1)),
        m1_s=dma((STAGES, Z)),
        m1_r=dma((STAGES, Z)),
        x1_s=dma((STAGES,)),
        x1_r=dma((STAGES,)),
        z1_s=dma((STAGES, Z)),
        z1_r=dma((STAGES, Z + 1)),
    )
    for s, plan in enumerate(LEVELS):
        tiles = (15, 6)[s]
        size = tile
        spaces[f"part{s}"] = pltpu.VMEM((tiles, tile, tile), f32)
        spaces[f"sum{s}"] = pltpu.VMEM((tiles, tile, tile), f32)
        for level, name in enumerate(plan):
            size //= COUNT[name]
            spaces[f"slot{s}_{level}"] = pltpu.VMEM((COUNT[name], tiles, size, tile), f32)
            if level + 1 < len(plan):
                spaces[f"held{s}_{level + 1}"] = pltpu.VMEM((tiles, size, tile), f32)
        for kind in ("ds", "dr", "us", "ur"):
            spaces[f"{kind}{s}"] = dma((len(plan), LANES))
    whole = pl.BlockSpec(memory_space=pl.ANY)
    vmem = pl.BlockSpec(memory_space=pltpu.VMEM)
    return pl.pallas_call(
        functools.partial(fused_kernel, tuple(spaces), width),
        out_shape=(
            jax.ShapeDtypeStruct((rows, all_cols), f32),
            jax.ShapeDtypeStruct((all_cols, all_cols), f32),
        ),
        in_specs=[whole, whole, whole, whole, pl.BlockSpec(memory_space=pltpu.SMEM)],
        out_specs=(vmem, vmem),
        scratch_shapes=list(spaces.values()),
        compiler_params=pltpu.CompilerParams(
            collective_id=0, has_side_effects=True, vmem_limit_bytes=63 * 2**20
        ),
    )(anc_inverse, anc_factor, win_factor, pivot_inverse, structure)


precise = lax.Precision.HIGHEST


def product(left, right):
    return jnp.dot(left, right, precision=precise, preferred_element_type=jnp.float32)


def on_device(anc_inverse, anc_factor, win_factor, pivot_inverse, structure):
    row_count = lax.axis_size("prow")
    col_count = lax.axis_size("pcol")
    steps, width = pivot_inverse.shape[:2]
    fits = steps == 3 and 2 * anc_factor.shape[0] == 3 * width and width % 256 == 0
    if row_count == 1 and col_count == 4 * Z and fits:
        return fused(anc_inverse, anc_factor, win_factor, pivot_inverse, structure)
    row_index = lax.axis_index("prow")
    col_index = lax.axis_index("pcol")
    block_rows = anc_inverse.shape[0]
    block_cols = anc_inverse.shape[1]
    steps_total = pivot_inverse.shape[0]
    width = pivot_inverse.shape[1]
    all_cols = anc_factor.shape[1]
    block_count = structure.shape[1]
    ratio_cols = col_count // row_count
    share_rows = block_rows // col_count
    structure_cols = structure.T.astype(jnp.float32)
    global_rows = col_index * block_cols + lax.iota(jnp.int32, block_cols)
    onehot_rows = (
        (global_rows // width)[:, None] == lax.iota(jnp.int32, block_count)[None, :]
    ).astype(jnp.float32)
    kept_rows = product(onehot_rows, structure_cols)
    share_offset = col_index * share_rows
    share_global = (row_index * col_count + col_index) * share_rows + lax.iota(
        jnp.int32, share_rows
    )
    onehot_share = (
        (share_global // width)[:, None] == lax.iota(jnp.int32, block_count)[None, :]
    ).astype(jnp.float32)
    kept_share = product(onehot_share, structure_cols)
    slot_ids = lax.iota(jnp.int32, col_count)
    source_flag = (slot_ids // row_count == col_index - row_index * ratio_cols).astype(jnp.float32)
    pieces = jnp.tile(anc_factor.reshape(row_count, share_rows, all_cols), (ratio_cols, 1, 1))
    outgoing = pieces * source_flag[:, None, None]
    incoming = lax.all_to_all(outgoing, "pcol", split_axis=0, concat_axis=0, tiled=True)
    factor_share = jnp.sum(incoming, axis=0)
    column_store = {}
    share_store = {}
    window_blocks = {}
    for k in range(steps_total - 1, -1, -1):
        first_col = k * width
        factor_now = anc_factor[:, first_col : first_col + width] * kept_rows[:, k : k + 1]
        share_factor = factor_share[:, first_col : first_col + width] * kept_share[:, k : k + 1]
        finished = list(range(k + 1, steps_total))
        if finished:
            stacked = jnp.concatenate([column_store[j] for j in finished], axis=1)
            factor_win = win_factor[first_col + width :, first_col : first_col + width]

        def term_rows(start, count, factor_now=factor_now):
            return product(anc_inverse, factor_now)

        share_image = lax.psum_scatter(
            term_rows(jnp.int32(0), share_rows * lax.axis_size("pcol")),
            "pcol",
            scatter_dimension=0,
            tiled=True,
        )
        if finished:
            share_image = share_image + product(
                lax.dynamic_slice_in_dim(stacked, share_offset, share_rows, 0), factor_win
            )
        share_column = -share_image
        column_now = lax.all_gather(share_column, "pcol", axis=0, tiled=True)
        crossings = [product(share_store[j].T, share_factor) for j in finished]
        pivot_part = product(share_factor.T, share_column)
        cross_sums = []
        if finished:
            cross_total = lax.psum(jnp.stack(crossings), ("prow", "pcol"))
            cross_sums = [cross_total[position] for position in range(len(finished))]
        pivot_sum = lax.psum(pivot_part, ("prow", "pcol"))
        for position, j in enumerate(finished):
            running = cross_sums[position]
            for i in finished:
                running = running + product(
                    window_blocks[j, i],
                    win_factor[i * width : (i + 1) * width, first_col : first_col + width],
                )
            window_blocks[j, k] = -running
            window_blocks[k, j] = -running.T
        pivot_block = pivot_inverse[k] - pivot_sum
        for j in finished:
            pivot_block = pivot_block - product(
                win_factor[j * width : (j + 1) * width, first_col : first_col + width].T,
                window_blocks[j, k],
            )
        window_blocks[k, k] = pivot_block
        column_store[k] = column_now
        share_store[k] = share_column
    anc_columns = jnp.concatenate([share_store[k] for k in range(steps_total)], axis=1)
    win_inverse = jnp.concatenate(
        [
            jnp.concatenate([window_blocks[i, k] for k in range(steps_total)], axis=1)
            for i in range(steps_total)
        ],
        axis=0,
    )
    return (anc_columns, win_inverse)


def solution(mesh):
    in_specs = (
        P(("pole", "prow"), "pcol"),
        P(("pole", "pcol"), None),
        P("pole", None),
        P("pole", None, None),
        P(),
    )
    out_specs = (P(("pole", "prow", "pcol"), None), P("pole", None))
    return jax.shard_map(
        on_device, mesh=mesh, in_specs=in_specs, out_specs=out_specs, check_vma=False
    )
```

```python
import functools

import jax
import jax.numpy as jnp
from jax import lax
from jax.experimental import pallas as pl
from jax.experimental.pallas import tpu as pltpu
from jax.sharding import PartitionSpec as P

MESH = pl.DeviceIdType.MESH
UP, DOWN, ACROSS, MATE = range(4)
Z = 4
LANES = 8


def split(value):
    high = value.astype(jnp.bfloat16)
    low = (value - high.astype(jnp.float32)).astype(jnp.bfloat16)
    return high, low


def dot3(left, right):
    (lh, ll), (rh, rl) = left, right
    dot = functools.partial(jnp.dot, preferred_element_type=jnp.float32)
    return dot(lh, rh) + (dot(lh, rl) + dot(ll, rh))


def mul(left, right):
    return dot3(split(left), split(right))


STAGES = 2
FIRST = (0, 9)
TOTAL = 17


def item_list(s, u):
    if u == 0:
        rest = [("R1", 3), ("R0", 3), ("R1", 2), ("R0", 2), ("R1", 1), ("R0", 1)]
        return [("G", 0), ("H", 0)] + rest
    far = [("X", 0)] if s == 0 else []
    if u == 1:
        rest = [("R1", 3)] + far + [("R0", 3), ("R1", 2), ("R0", 2)]
        return [("G", 1), ("H", 1), ("G", 0), ("H", 0)] + rest
    rest = [("G", 1), ("H", 1), ("G", 0), ("H", 0), ("R1", 3)] + far + [("R0", 3)]
    return [("G", 2), ("H", 2)] + rest


def item_at(u, n):
    s = 1 if n >= FIRST[1] else 0
    items = item_list(s, u)
    n -= FIRST[s]
    return (s, *items[n]) if n < len(items) else (s, "", 0)


X_SENDS = {
    1: ("G", 0, 1), 2: ("F", 0, 2), 3: ("G", 0, 2), 4: ("F", 0, 1), 5: ("F", 0, 0), 7: ("F", 1, 3), 8: ("R", 0, 0),
    9: ("F", 1, 2), 10: ("G", 1, 1), 11: ("F", 1, 1), 12: ("G", 1, 2), 13: ("F", 1, 0), 14: ("G", 1, 3), 16: ("R", 1, 0),
}
X_TAKES = {2: (0, 0), 3: (0, 1), 5: (0, 2), 9: (1, 0), 12: (1, 1), 14: (1, 2), 16: (1, 3)}


def order_static(z):
    return ([0, 1, 2, 3], [1, 0, 2, 3], [2, 3, 1, 0], [3, 2, 1, 0])[z]


def fused_kernel(names, width, anc_ref, fac_ref, win_ref, piv_ref, str_ref, cols_hbm, out_hbm, *scratch):
    m = dict(zip(names, scratch, strict=True))
    cols_ref, out_ref = m["cols"], m["out"]
    fac, a_buf, win_st, piv_st = m["fac"], m["a_buf"], m["win"], m["piv"]
    lr_hi, lr_lo, lt_hi, lt_lo = m["lr_hi"], m["lr_lo"], m["lt_hi"], m["lt_lo"]
    tr_hi, tr_lo = m["tr_hi"], m["tr_lo"]
    own, near, y_own, y_near = m["own"], m["near"], m["y_own"], m["y_near"]
    p0, m0i, x0i, z0i = m["p0"], m["m0i"], m["x0i"], m["z0i"]
    p1, m1i, x1i, z1i = m["p1"], m["m1i"], m["x1i"], m["z1i"]

    me = lax.axis_index("pcol")
    core = lax.rem(me, 2)
    x = lax.rem(me // 2, 2)
    z = me // 4
    lane = me // 2
    rows = fac.shape[0]
    tile = width // 2
    mate = me + 1 - 2 * core

    def index(zz, xx, cc):
        return (zz * 2 + xx) * 2 + cc

    x_other = 1 - x
    across = index(z, x_other, core)

    def order(t):
        inner = (0, 0, 2, 3) if t else (1, 1, 1, 1)
        lowmid = inner[t] if t else 1
        highmid = 3 - lowmid
        return jnp.where(z == 0, t, jnp.where(z == 1, lowmid, jnp.where(z == 2, highmid, 3 - t)))

    def job_chip(q):
        return order(3 - q // 2) * 2 + (1 - x if q % 2 == 0 else x)

    def load_anc(q):
        at = pl.ds(pl.multiple_of(job_chip(q) * 2 * rows, 2 * rows), 2 * rows)
        return pltpu.make_async_copy(anc_ref.at[at, :], a_buf.at[q % 4], m["load_sem"].at[q])

    load_fac = pltpu.make_async_copy(fac_ref, fac, m["load_sem"].at[8])
    load_piv = pltpu.make_async_copy(piv_ref, piv_st, m["load_sem"].at[9])
    win_pairs = [(2, 1), (1, 0), (2, 0)]

    def load_win(n):
        j, k = win_pairs[n]
        block = win_ref.at[pl.ds(j * width, width), pl.ds(k * width, width)]
        return pltpu.make_async_copy(block, win_st.at[n], m["load_sem"].at[10 + n])

    load_fac.start()
    for q in range(4):
        load_anc(q).start()

    barrier = pltpu.get_barrier_semaphore()
    for d in range(1, LANES):
        peer = lax.rem(lane + d, LANES) * 2 + core
        pl.semaphore_signal(barrier, inc=1, device_id={"pcol": peer}, device_id_type=MESH)
    pl.semaphore_signal(barrier, inc=1, device_id={"pcol": mate}, device_id_type=MESH)

    common = []
    by_z = [[] for _ in range(Z)]
    log = [common]

    def go(make):
        make().start()
        log[0].append(make)

    def remote(src, dst, ssem, rsem, dest):
        return pltpu.make_async_remote_copy(
            src_ref=src, dst_ref=dst, send_sem=ssem, recv_sem=rsem, device_id={"pcol": dest}, device_id_type=MESH
        )

    def arrive(dst, rsem):
        remote(dst, dst, rsem, rsem, mate).wait_recv()

    def core_rows(c):
        return pl.ds(pl.multiple_of(c * rows, rows), rows)

    def own_at(s, zz, xx, c):
        return own.at[s, zz * 2 + xx, core_rows(c), :]

    def near_at(s, zz, c):
        return near.at[s, zz, core_rows(c), :]

    def own_send(s, zz, xx, kind, dest):
        def make():
            ref = own_at(s, zz, xx, core)
            return remote(ref, ref, m["own_s"].at[s, kind, zz * 2 + xx], m["own_r"].at[s, zz * 2 + xx, core], dest)
        go(make)

    def near_send(s, zz, kind, dest):
        def make():
            ref = near_at(s, zz, core)
            return remote(ref, ref, m["near_s"].at[s, kind, zz], m["near_r"].at[s, zz, core], dest)
        go(make)

    def own_wait(s, zz, xx, c):
        arrive(own_at(s, zz, xx, c), m["own_r"].at[s, zz * 2 + xx, c])

    def near_wait(s, zz, c):
        arrive(near_at(s, zz, c), m["near_r"].at[s, zz, c])

    def columns(t):
        return slice(t * tile, (t + 1) * tile)

    def mask(t):
        for piece in range(rows // tile):
            block = (me * (rows // tile) + piece) // 2
            kept = str_ref[t // 2, block].astype(jnp.float32)
            at = slice(piece * tile, (piece + 1) * tile)
            fac[at, columns(t)] = fac[at, columns(t)] * kept

    own_tiles, near_tiles, sum_tiles = (5, 2), (4, 1), (3, 0)

    load_fac.wait()
    mask(own_tiles[0])
    own[0, lane, core_rows(core), :] = fac[:, columns(own_tiles[0])]
    pl.semaphore_wait(barrier, LANES)

    def in_direction(direction, zz):
        return zz if direction == UP else Z - 1 - zz

    z_dests = (me + 4, me - 4)

    def z_dest(direction):
        return z_dests[direction]

    def landing(direction, zz, dest_z):
        return Z if direction == DOWN and dest_z == zz else dest_z

    def z_send(direction, zz, n):
        s, kind, v = item_at(in_direction(direction, zz), n)
        vz = in_direction(direction, v)
        first = in_direction(direction, zz) == 0
        dest = z_dest(direction)
        there = zz + 1 if direction == UP else zz - 1
        if kind == "G":
            own_send(s, vz, x, direction, dest)
        elif kind == "H":
            near_send(s, vz, direction, dest)
        elif kind == "X":
            own_send(s, vz, x_other, direction, dest)
        elif kind == "R1":
            arrive(m1i.at[s, vz], m["m1_r"].at[s, vz])
            value = p1[s, 0, vz] + m1i[s, vz]
            if not first:
                value = value + z1i[s, vz]
            p1[s, 0, vz] = value
            at = landing(direction, there, vz)
            go(lambda: remote(p1.at[s, 0, vz], z1i.at[s, at], m["z1_s"].at[s, vz], m["z1_r"].at[s, at], z_dest(direction)))
        elif kind == "R0":
            arrive(m0i.at[s, 0, vz], m["m0_r"].at[s, 0, vz])
            arrive(x0i.at[s, vz], m["x0_r"].at[s, vz])
            value = p0[s, 0, 0, vz] + m0i[s, 0, vz] + x0i[s, vz]
            if not first:
                value = value + z0i[s, vz]
            p0[s, 0, 0, vz] = value
            at = landing(direction, there, vz)
            go(lambda: remote(p0.at[s, 0, 0, vz], z0i.at[s, at], m["z0_s"].at[s, vz], m["z0_r"].at[s, at], z_dest(direction)))

    def z_arrival(direction, zz, n):
        u = in_direction(direction, zz)
        s, kind, v = item_at(u - 1, n)
        vz = in_direction(direction, v)
        if kind == "G":
            own_wait(s, vz, x, core)
            own_send(s, vz, x, MATE, mate)
        elif kind == "H":
            near_wait(s, vz, core)
            near_send(s, vz, MATE - 1, mate)
        elif kind == "X":
            own_wait(s, vz, x_other, core)
            own_send(s, vz, x_other, MATE, mate)
        elif kind == "R1":
            at = landing(direction, zz, vz)
            arrive(z1i.at[s, at], m["z1_r"].at[s, at])
        elif kind == "R0":
            at = landing(direction, zz, vz)
            arrive(z0i.at[s, at], m["z0_r"].at[s, at])

    def x_sum(s, v):
        arrive(m0i.at[s, 1, v], m["m0_r"].at[s, 1, v])
        p0[s, 0, 1, v] = p0[s, 0, 1, v] + m0i[s, 1, v]
        go(lambda: remote(p0.at[s, 0, 1, v], x0i.at[s, v], m["x0_s"].at[s, v], m["x0_r"].at[s, v], across))

    def x_near(s, zz):
        arrive(m1i.at[s, zz], m["m1_r"].at[s, zz])
        value = p1[s, 0, zz] + m1i[s, zz]
        if zz > 0:
            value = value + z1i[s, zz]
        if zz < Z - 1:
            value = value + z1i[s, Z]
        p1[s, 0, zz] = value
        go(lambda: remote(p1.at[s, 0, zz], x1i.at[s], m["x1_s"].at[s], m["x1_r"].at[s], across))

    def x_step(kind, s, t, zz):
        v = order_static(zz)[t]
        if kind == "G":
            own_send(s, v, x, ACROSS, across)
        elif kind == "F":
            x_sum(s, v)
        else:
            x_near(s, zz)

    def x_arrival(s, t, zz):
        v = order_static(zz)[t]
        own_wait(s, v, x_other, core)
        own_send(s, v, x_other, MATE, mate)

    def events(step):
        for zz in range(Z):
            log[0] = by_z[zz]

            @pl.when(z == zz)
            def _():
                for direction in (UP, DOWN):
                    if in_direction(direction, zz) > 0 and 0 <= step - 1 < TOTAL:
                        z_arrival(direction, zz, step - 1)
                for direction in (UP, DOWN):
                    if in_direction(direction, zz) < Z - 1 and 2 <= step + 1 < TOTAL:
                        z_send(direction, zz, step + 1)
                if step in X_SENDS:
                    x_step(*X_SENDS[step], zz)
                if step in X_TAKES:
                    x_arrival(*X_TAKES[step], zz)

            log[0] = common

    def begin(s):
        own_send(s, z, x, ACROSS, across)
        own_send(s, z, x, MATE, mate)
        near_send(s, z, MATE - 1, mate)

    for zz in range(Z):
        log[0] = by_z[zz]

        @pl.when(z == zz)
        def _():
            for direction in (UP, DOWN):
                if in_direction(direction, zz) < Z - 1:
                    z_send(direction, zz, 0)

        log[0] = common
    own_send(0, z, x, ACROSS, across)
    own_send(0, z, x, MATE, mate)

    mask(near_tiles[0])
    near[0, z, core_rows(core), :] = fac[:, columns(near_tiles[0])]
    near_send(0, z, MATE - 1, mate)
    for zz in range(Z):
        log[0] = by_z[zz]

        @pl.when(z == zz)
        def _():
            for direction in (UP, DOWN):
                if in_direction(direction, zz) < Z - 1:
                    z_send(direction, zz, 1)

        log[0] = common

    for t in (sum_tiles[0], sum_tiles[1], near_tiles[1], own_tiles[1]):
        mask(t)
    for n, t in enumerate((sum_tiles[0], sum_tiles[1], near_tiles[0], near_tiles[1])):
        high, low = split(fac[:, columns(t)])
        lr_hi[:, columns(n)] = high
        lr_lo[:, columns(n)] = low

    def chip_job(q):
        v = order(3 - q // 2)
        other = q % 2 == 0
        side = 1 if other else 0
        chip = job_chip(q)
        load_anc(q).wait()

        def both(i, carry):
            c = core + (1 - 2 * core) * (1 - i)
            pair = split(a_buf[q % 4, core_rows(c), :])
            count = (4 if other else 2) * tile
            value = dot3(pair, (lr_hi[:, :count], lr_lo[:, :count]))
            for s in range(STAGES):
                p0[s, 1 - i, side, v] = value[:, columns(s)]
                if other:
                    p1[s, 1 - i, v] = value[:, columns(2 + s)]
            return carry

        lax.fori_loop(0, 2, both, 0)
        for s in range(STAGES):
            go(lambda s=s: remote(p0.at[s, 1, side, v], m0i.at[s, side, v], m["m0_s"].at[s, side, v], m["m0_r"].at[s, side, v], mate))
            if other:
                go(lambda s=s: remote(p1.at[s, 1, v], m1i.at[s, v], m["m1_s"].at[s, v], m["m1_r"].at[s, v], mate))

        def flip(c, carry):
            high, low = split(a_buf[q % 4, core_rows(c), :].T)
            at = pl.ds(pl.multiple_of(c * rows, rows), rows)
            tr_hi[chip, :, at] = high
            tr_lo[chip, :, at] = low
            return carry

        lax.fori_loop(0, 2, flip, 0)
        if q + 4 < 8:
            load_anc(q + 4).start()

    def pair_job(block, total, chip, first):
        high, low = split(block)
        left, rest = tr_hi[chip], tr_lo[chip]
        wide = jnp.dot(left, jnp.concatenate([high, low], axis=1), preferred_element_type=jnp.float32)
        value = wide[:, :tile] + (wide[:, tile:] + jnp.dot(rest, high, preferred_element_type=jnp.float32))
        if first:
            total[...] = value
        else:
            total[...] += value

    def own_job(s, t, other):
        zz = order(t)
        xx = 1 - x if other else x
        own_wait(s, zz, xx, 1 - core)
        pair_job(own[s, zz * 2 + xx], y_own.at[s], zz * 2 + xx, t == 0 and not other)

    def near_job(s, t):
        zz = order(t)
        near_wait(s, zz, 1 - core)
        pair_job(near[s, zz], y_near.at[s], zz * 2 + x, t == 0)

    def finish_own(s):
        cols_ref[:, columns(own_tiles[s])] = y_own[s]

    def finish(s):
        arrive(x1i.at[s], m["x1_r"].at[s])
        cols_ref[:, columns(near_tiles[s])] = y_near[s] + x1i[s]
        arrive(m0i.at[s, 0, z], m["m0_r"].at[s, 0, z])
        arrive(x0i.at[s, z], m["x0_r"].at[s, z])
        value = p0[s, 0, 0, z] + m0i[s, 0, z] + x0i[s, z]
        low = z0i[s, z]
        high = z0i[s, Z]
        value = value + jnp.where(z > 0, low, 0.0) + jnp.where(z < Z - 1, high, 0.0)
        cols_ref[:, columns(sum_tiles[s])] = value

    half_cols = 3 * tile
    sum_list = (
        [(q, p) for q in (3, 4, 5) for p in range(q + 1)],
        [(2, p) for p in range(3)],
        [(q, p) for q in (0, 1) for p in range(q + 1)],
    )

    def inner_early():
        flipped = split(cols_ref[:, half_cols:].T)
        value = dot3(flipped, split(fac[...]))
        for n, (q, p) in enumerate(sum_list[0]):
            m["part0"][n] = value[(q - 3) * tile : (q - 2) * tile, columns(p)]

    def inner_middle():
        value = dot3(split(cols_ref[:, columns(2)].T), split(fac[:, :half_cols]))
        for n, (q, p) in enumerate(sum_list[1]):
            m["part1"][n] = value[:, columns(p)]

    def inner_late():
        value = dot3((lt_hi[:width, :], lt_lo[:width, :]), split(cols_ref[:, :width]))
        for n, (q, p) in enumerate(sum_list[2]):
            m["part2"][n] = value[columns(q), columns(p)]

    groups = {
        "mate": (2, core, lambda n: index(z, x, n)),
        "x": (2, x, lambda n: index(z, n, core)),
        "z": (Z, z, lambda n: index(n, x, core)),
        "lane": (LANES, lane, lambda n: n * 2 + core),
    }

    def reducer(s):
        plan = LEVELS[s]
        sums = m[f"sum{s}"]
        sizes = [tile]
        for name in plan:
            sizes.append(sizes[-1] // groups[name][0])
        base = [0]
        for name, size in zip(plan, sizes[1:]):
            base.append(base[-1] + groups[name][1] * size)

        def held(level):
            return m[f"part{s}"] if level == 0 else m[f"held{s}_{level}"]

        def peer_of(level, d):
            count, mine, _ = groups[plan[level]]
            return 1 - mine if count == 2 else lax.rem(mine + d, count)

        def send_down(level):
            count, mine, device = groups[plan[level]]
            size = sizes[level + 1]
            for d in range(1, count):
                def make(d=d):
                    peer = peer_of(level, d)
                    src = held(level).at[:, pl.ds(pl.multiple_of(peer * size, size), size), :]
                    return remote(
                        src, m[f"slot{s}_{level}"].at[mine], m[f"ds{s}"].at[level, peer], m[f"dr{s}"].at[level, mine], device(peer)
                    )
                go(make)

        def take_down(level):
            count, mine, device = groups[plan[level]]
            size = sizes[level + 1]
            slot = m[f"slot{s}_{level}"]
            total = held(level)[:, pl.ds(pl.multiple_of(mine * size, size), size), :]
            for d in range(1, count):
                peer = peer_of(level, d)
                arrive(slot.at[peer], m[f"dr{s}"].at[level, peer])
                total = total + slot[peer]
            if level + 1 < len(plan):
                held(level + 1)[...] = total
            else:
                sums[:, pl.ds(pl.multiple_of(base[-1], size), size), :] = total

        def part_at(level, owner):
            size = sizes[level + 1]
            return sums.at[:, pl.ds(pl.multiple_of(base[level] + owner * size, size), size), :]

        def send_up(level):
            count, mine, device = groups[plan[level]]
            for d in range(1, count):
                def make(d=d):
                    peer = peer_of(level, d)
                    ref = part_at(level, mine)
                    return remote(ref, ref, m[f"us{s}"].at[level, peer], m[f"ur{s}"].at[level, mine], device(peer))
                go(make)

        def take_up(level):
            count, mine, device = groups[plan[level]]
            for d in range(1, count):
                peer = peer_of(level, d)
                arrive(part_at(level, peer), m[f"ur{s}"].at[level, peer])

        steps = [lambda: send_down(0)]
        for level in range(len(plan)):
            def step(level=level):
                take_down(level)
                if level + 1 < len(plan):
                    send_down(level + 1)
                else:
                    send_up(level)
            steps.append(step)
        for level in range(len(plan) - 1, -1, -1):
            def step(level=level):
                take_up(level)
                if level > 0:
                    send_up(level - 1)
            steps.append(step)
        return steps

    inner = m["inner"]
    blocks = [(2, 2), (2, 1), (2, 0), (1, 1), (1, 0), (0, 0)]

    def place(s):
        for n, (q, p) in enumerate(sum_list[s]):
            value = m[f"sum{s}"][n]
            at = blocks.index((q // 2, p // 2))
            inner[at, (q % 2) * tile : (q % 2 + 1) * tile, (p % 2) * tile : (p % 2 + 1) * tile] = value
            if q // 2 == p // 2 and q != p:
                inner[at, (p % 2) * tile : (p % 2 + 1) * tile, (q % 2) * tile : (q % 2 + 1) * tile] = value.T

    def n_block(j, k):
        return inner[blocks.index((j, k))]

    def fac_block(j, k):
        return win_st[win_pairs.index((j, k))]

    def save_block(j, k):
        block = out_ref.at[pl.ds(j * width, width), pl.ds(k * width, width)]
        target = out_hbm.at[pl.ds(j * width, width), pl.ds(k * width, width)]
        return pltpu.make_async_copy(block, target, m["save_sem"].at[j, k])

    def save_column(k):
        at = pl.ds(k * width, width)
        return pltpu.make_async_copy(cols_ref.at[:, at], cols_hbm.at[:, at], m["save_sem"].at[3, k])

    def put(j, k, value):
        out_ref[j * width : (j + 1) * width, k * width : (k + 1) * width] = value
        save_block(j, k).start()

    def got(j, k):
        return out_ref[j * width : (j + 1) * width, k * width : (k + 1) * width]

    early = m["early"]

    def window_first():
        put(2, 2, piv_st[2] + n_block(2, 2))
        value = n_block(2, 1) - mul(got(2, 2), fac_block(2, 1))
        put(2, 1, value)
        put(1, 2, value.T)
        value = n_block(2, 0) - mul(got(2, 1), fac_block(1, 0)) - mul(got(2, 2), fac_block(2, 0))
        put(2, 0, value)
        put(0, 2, value.T)

    def window_second():
        flip21 = split(fac_block(2, 1).T)
        known = piv_st[1] - mul(n_block(2, 1).T, fac_block(2, 1)) - dot3(flip21, split(got(2, 1)))
        early[0] = known
        turned = dot3(flip21, split(n_block(2, 0)))
        left = jnp.concatenate([fac_block(2, 1).T, known, got(1, 2)], axis=1)
        right = jnp.concatenate([n_block(2, 0), fac_block(1, 0), fac_block(2, 0)], axis=0)
        early[1] = mul(left, right)
        early[2] = (
            piv_st[0]
            + mul(turned.T, fac_block(1, 0))
            - mul(n_block(2, 0).T, fac_block(2, 0))
            - mul(fac_block(2, 0).T, got(2, 0))
        )

    def window_last():
        put(1, 1, early[0] + n_block(1, 1))
        value = n_block(1, 0) - early[1] - mul(n_block(1, 1), fac_block(1, 0))
        put(1, 0, value)
        put(0, 1, value.T)
        put(0, 0, early[2] + n_block(0, 0) - mul(n_block(1, 0).T, fac_block(1, 0)) - mul(fac_block(1, 0).T, value))

    def column(k):
        return cols_ref[:, k * width : (k + 1) * width]

    def put_column(k):
        value = column(k)
        for j in range(k + 1, 3):
            value = value + mul(column(j), fac_block(j, k))
        cols_ref[:, k * width : (k + 1) * width] = -value

    chip_job(0)
    chip_job(1)
    x_sum(0, order(3))
    load_piv.start()
    for n in range(3):
        load_win(n).start()
    events(1)
    chip_job(2)
    chip_job(3)
    events(2)
    chip_job(4)
    chip_job(5)
    own[1, lane, core_rows(core), :] = fac[:, columns(own_tiles[1])]
    near[1, z, core_rows(core), :] = fac[:, columns(near_tiles[1])]
    events(3)
    chip_job(6)
    chip_job(7)
    events(4)
    own_job(0, 0, False)
    own_job(0, 1, False)
    events(5)
    near_job(0, 0)
    near_job(0, 1)
    own_job(0, 0, True)
    own_job(0, 1, True)
    events(6)
    begin(1)
    own_job(0, 2, False)
    near_job(0, 2)
    own_job(0, 2, True)
    events(7)
    own_job(0, 3, False)
    high, low = split(fac[:, :half_cols].T)
    lt_hi[...] = high
    lt_lo[...] = low
    events(8)
    near_job(0, 3)
    events(9)
    own_job(0, 3, True)
    events(10)
    finish_own(0)
    finish(0)
    inner_early()
    cols_ref[:, 2 * width :] = -cols_ref[:, 2 * width :]
    save_column(2).start()
    first, middle, last = reducer(0), reducer(1), reducer(2)
    first[0]()
    own_job(1, 0, False)
    first[1]()
    events(11)
    own_job(1, 1, False)
    near_job(1, 0)
    near_job(1, 1)
    own_job(1, 0, True)
    events(12)
    first[2]()
    events(13)
    first[3]()
    own_job(1, 1, True)
    own_job(1, 2, False)
    near_job(1, 2)
    events(14)
    first[4]()
    own_job(1, 2, True)
    load_piv.wait()
    for n in range(3):
        load_win(n).wait()
    events(15)
    first[5]()
    own_job(1, 3, False)
    events(16)
    near_job(1, 3)
    own_job(1, 3, True)
    finish_own(1)
    inner_middle()
    middle[0]()
    first[6]()
    place(0)
    window_first()
    middle[1]()
    events(17)
    finish(1)
    inner_late()
    last[0]()
    middle[2]()
    window_second()
    last[1]()
    middle[3]()
    put_column(1)
    save_column(1).start()
    last[2]()
    middle[4]()
    put_column(0)
    save_column(0).start()
    for step in last[3:]:
        step()
    place(1)
    place(2)
    window_last()
    for k in range(3):
        save_column(k).wait()
        for j in range(3):
            save_block(j, k).wait()

    for make in common:
        make().wait_send()
    for zz in range(Z):

        @pl.when(z == zz)
        def _():
            for make in by_z[zz]:
                make().wait_send()


LEVELS = (("mate", "x", "z"), ("mate", "lane"), ("mate", "lane"))
COUNT = dict(mate=2, x=2, z=Z, lane=LANES)


def fused(anc_inverse, anc_factor, win_factor, pivot_inverse, structure):
    steps, width = pivot_inverse.shape[:2]
    rows, all_cols = anc_factor.shape
    tile = width // 2
    f32, b16 = jnp.float32, jnp.bfloat16
    dma = pltpu.SemaphoreType.DMA
    block = (rows, tile)
    pair = (2 * rows, tile)
    spaces = dict(
        cols=pltpu.VMEM((rows, all_cols), f32),
        out=pltpu.VMEM((all_cols, all_cols), f32),
        save_sem=dma((4, 3)),
        fac=pltpu.VMEM((rows, all_cols), f32),
        a_buf=pltpu.VMEM((4, 2 * rows, rows), f32),
        win=pltpu.VMEM((3, width, width), f32),
        piv=pltpu.VMEM(pivot_inverse.shape, f32),
        lr_hi=pltpu.VMEM((rows, 4 * tile), b16),
        lr_lo=pltpu.VMEM((rows, 4 * tile), b16),
        lt_hi=pltpu.VMEM((3 * tile, rows), b16),
        lt_lo=pltpu.VMEM((3 * tile, rows), b16),
        tr_hi=pltpu.VMEM((LANES, rows, 2 * rows), b16),
        tr_lo=pltpu.VMEM((LANES, rows, 2 * rows), b16),
        own=pltpu.VMEM((STAGES, LANES, *pair), f32),
        near=pltpu.VMEM((STAGES, Z, *pair), f32),
        y_own=pltpu.VMEM((STAGES, *block), f32),
        y_near=pltpu.VMEM((STAGES, *block), f32),
        p0=pltpu.VMEM((STAGES, 2, 2, Z, *block), f32),
        m0i=pltpu.VMEM((STAGES, 2, Z, *block), f32),
        x0i=pltpu.VMEM((STAGES, Z, *block), f32),
        z0i=pltpu.VMEM((STAGES, Z + 1, *block), f32),
        p1=pltpu.VMEM((STAGES, 2, Z, *block), f32),
        m1i=pltpu.VMEM((STAGES, Z, *block), f32),
        x1i=pltpu.VMEM((STAGES, *block), f32),
        z1i=pltpu.VMEM((STAGES, Z + 1, *block), f32),
        inner=pltpu.VMEM((6, width, width), f32),
        early=pltpu.VMEM((3, width, width), f32),
        load_sem=dma((13,)),
        own_s=dma((STAGES, 4, LANES)),
        own_r=dma((STAGES, LANES, 2)),
        near_s=dma((STAGES, 3, Z)),
        near_r=dma((STAGES, Z, 2)),
        m0_s=dma((STAGES, 2, Z)),
        m0_r=dma((STAGES, 2, Z)),
        x0_s=dma((STAGES, Z)),
        x0_r=dma((STAGES, Z)),
        z0_s=dma((STAGES, Z)),
        z0_r=dma((STAGES, Z + 1)),
        m1_s=dma((STAGES, Z)),
        m1_r=dma((STAGES, Z)),
        x1_s=dma((STAGES,)),
        x1_r=dma((STAGES,)),
        z1_s=dma((STAGES, Z)),
        z1_r=dma((STAGES, Z + 1)),
    )
    for s, plan in enumerate(LEVELS):
        tiles = (15, 3, 3)[s]
        size = tile
        spaces[f"part{s}"] = pltpu.VMEM((tiles, tile, tile), f32)
        spaces[f"sum{s}"] = pltpu.VMEM((tiles, tile, tile), f32)
        for level, name in enumerate(plan):
            size //= COUNT[name]
            spaces[f"slot{s}_{level}"] = pltpu.VMEM((COUNT[name], tiles, size, tile), f32)
            if level + 1 < len(plan):
                spaces[f"held{s}_{level + 1}"] = pltpu.VMEM((tiles, size, tile), f32)
        for kind in ("ds", "dr", "us", "ur"):
            spaces[f"{kind}{s}"] = dma((len(plan), LANES))
    whole = pl.BlockSpec(memory_space=pl.ANY)
    return pl.pallas_call(
        functools.partial(fused_kernel, tuple(spaces), width),
        out_shape=(
            jax.ShapeDtypeStruct((rows, all_cols), f32),
            jax.ShapeDtypeStruct((all_cols, all_cols), f32),
        ),
        in_specs=[whole, whole, whole, whole, pl.BlockSpec(memory_space=pltpu.SMEM)],
        out_specs=(whole, whole),
        scratch_shapes=list(spaces.values()),
        compiler_params=pltpu.CompilerParams(
            collective_id=0, has_side_effects=True, vmem_limit_bytes=63 * 2**20
        ),
    )(anc_inverse, anc_factor, win_factor, pivot_inverse, structure)


def land_kernel(parts, *refs):
    count = len(parts)
    sources, targets = refs[:count], refs[count : 2 * count]
    held, sem = refs[2 * count : 3 * count], refs[3 * count]
    copies = []
    for n, pieces in enumerate(parts):
        size = sources[n].shape[0] // pieces
        for i in range(pieces):
            at = pl.ds(i * size, size)
            read = pltpu.make_async_copy(sources[n].at[at, :], held[n].at[at, :], sem.at[0, len(copies)])
            write = pltpu.make_async_copy(held[n].at[at, :], targets[n].at[at, :], sem.at[1, len(copies)])
            read.start()
            copies.append((read, write))
    for read, write in copies:
        read.wait()
        write.start()
    for read, write in copies:
        write.wait()


def land(*arrays):
    whole = pl.BlockSpec(memory_space=pl.ANY)
    parts = (3, 6)
    return pl.pallas_call(
        functools.partial(land_kernel, parts),
        out_shape=tuple(jax.ShapeDtypeStruct(a.shape, a.dtype) for a in arrays),
        in_specs=[whole] * len(arrays),
        out_specs=(whole,) * len(arrays),
        scratch_shapes=[pltpu.VMEM(a.shape, a.dtype) for a in arrays] + [pltpu.SemaphoreType.DMA((2, sum(parts)))],
    )(*arrays)


precise = lax.Precision.HIGHEST


def product(left, right):
    return jnp.dot(left, right, precision=precise, preferred_element_type=jnp.float32)


def on_device(anc_inverse, anc_factor, win_factor, pivot_inverse, structure):
    row_count = lax.axis_size("prow")
    col_count = lax.axis_size("pcol")
    steps, width = pivot_inverse.shape[:2]
    fits = steps == 3 and 2 * anc_factor.shape[0] == 3 * width and width % 256 == 0
    if row_count == 1 and col_count == 4 * Z and fits:
        return land(*fused(anc_inverse, anc_factor, win_factor, pivot_inverse, structure))
    row_index = lax.axis_index("prow")
    col_index = lax.axis_index("pcol")
    block_rows = anc_inverse.shape[0]
    block_cols = anc_inverse.shape[1]
    steps_total = pivot_inverse.shape[0]
    width = pivot_inverse.shape[1]
    all_cols = anc_factor.shape[1]
    block_count = structure.shape[1]
    ratio_cols = col_count // row_count
    share_rows = block_rows // col_count
    structure_cols = structure.T.astype(jnp.float32)
    global_rows = col_index * block_cols + lax.iota(jnp.int32, block_cols)
    onehot_rows = (
        (global_rows // width)[:, None] == lax.iota(jnp.int32, block_count)[None, :]
    ).astype(jnp.float32)
    kept_rows = product(onehot_rows, structure_cols)
    share_offset = col_index * share_rows
    share_global = (row_index * col_count + col_index) * share_rows + lax.iota(
        jnp.int32, share_rows
    )
    onehot_share = (
        (share_global // width)[:, None] == lax.iota(jnp.int32, block_count)[None, :]
    ).astype(jnp.float32)
    kept_share = product(onehot_share, structure_cols)
    slot_ids = lax.iota(jnp.int32, col_count)
    source_flag = (slot_ids // row_count == col_index - row_index * ratio_cols).astype(jnp.float32)
    pieces = jnp.tile(anc_factor.reshape(row_count, share_rows, all_cols), (ratio_cols, 1, 1))
    outgoing = pieces * source_flag[:, None, None]
    incoming = lax.all_to_all(outgoing, "pcol", split_axis=0, concat_axis=0, tiled=True)
    factor_share = jnp.sum(incoming, axis=0)
    column_store = {}
    share_store = {}
    window_blocks = {}
    for k in range(steps_total - 1, -1, -1):
        first_col = k * width
        factor_now = anc_factor[:, first_col : first_col + width] * kept_rows[:, k : k + 1]
        share_factor = factor_share[:, first_col : first_col + width] * kept_share[:, k : k + 1]
        finished = list(range(k + 1, steps_total))
        if finished:
            stacked = jnp.concatenate([column_store[j] for j in finished], axis=1)
            factor_win = win_factor[first_col + width :, first_col : first_col + width]

        def term_rows(start, count, factor_now=factor_now):
            return product(anc_inverse, factor_now)

        share_image = lax.psum_scatter(
            term_rows(jnp.int32(0), share_rows * lax.axis_size("pcol")),
            "pcol",
            scatter_dimension=0,
            tiled=True,
        )
        if finished:
            share_image = share_image + product(
                lax.dynamic_slice_in_dim(stacked, share_offset, share_rows, 0), factor_win
            )
        share_column = -share_image
        column_now = lax.all_gather(share_column, "pcol", axis=0, tiled=True)
        crossings = [product(share_store[j].T, share_factor) for j in finished]
        pivot_part = product(share_factor.T, share_column)
        cross_sums = []
        if finished:
            cross_total = lax.psum(jnp.stack(crossings), ("prow", "pcol"))
            cross_sums = [cross_total[position] for position in range(len(finished))]
        pivot_sum = lax.psum(pivot_part, ("prow", "pcol"))
        for position, j in enumerate(finished):
            running = cross_sums[position]
            for i in finished:
                running = running + product(
                    window_blocks[j, i],
                    win_factor[i * width : (i + 1) * width, first_col : first_col + width],
                )
            window_blocks[j, k] = -running
            window_blocks[k, j] = -running.T
        pivot_block = pivot_inverse[k] - pivot_sum
        for j in finished:
            pivot_block = pivot_block - product(
                win_factor[j * width : (j + 1) * width, first_col : first_col + width].T,
                window_blocks[j, k],
            )
        window_blocks[k, k] = pivot_block
        column_store[k] = column_now
        share_store[k] = share_column
    anc_columns = jnp.concatenate([share_store[k] for k in range(steps_total)], axis=1)
    win_inverse = jnp.concatenate(
        [
            jnp.concatenate([window_blocks[i, k] for k in range(steps_total)], axis=1)
            for i in range(steps_total)
        ],
        axis=0,
    )
    return (anc_columns, win_inverse)


def solution(mesh):
    in_specs = (
        P(("pole", "prow"), "pcol"),
        P(("pole", "pcol"), None),
        P("pole", None),
        P("pole", None, None),
        P(),
    )
    out_specs = (P(("pole", "prow", "pcol"), None), P("pole", None))
    return jax.shard_map(
        on_device, mesh=mesh, in_specs=in_specs, out_specs=out_specs, check_vma=False
    )
```

```python
import functools

import jax
import jax.numpy as jnp
from jax import lax
from jax.experimental import pallas as pl
from jax.experimental.pallas import tpu as pltpu
from jax.sharding import PartitionSpec as P

MESH = pl.DeviceIdType.MESH
UP, DOWN, ACROSS, MATE = range(4)
Z = 4
LANES = 8


def split(value):
    high = value.astype(jnp.bfloat16)
    low = (value - high.astype(jnp.float32)).astype(jnp.bfloat16)
    return high, low


def dot3(left, right):
    (lh, ll), (rh, rl) = left, right
    dot = functools.partial(jnp.dot, preferred_element_type=jnp.float32)
    return dot(lh, rh) + (dot(lh, rl) + dot(ll, rh))


def mul(left, right):
    return dot3(split(left), split(right))


STAGES = 2
FIRST = (0, 9)
TOTAL = 17


def item_list(s, u):
    if u == 0:
        rest = [("R1", 3), ("R0", 3), ("R1", 2), ("R0", 2), ("R1", 1), ("R0", 1)]
        return [("G", 0), ("H", 0)] + rest
    far = [("X", 0)] if s == 0 else []
    if u == 1:
        rest = [("R1", 3)] + far + [("R0", 3), ("R1", 2), ("R0", 2)]
        return [("G", 1), ("H", 1), ("G", 0), ("H", 0)] + rest
    rest = [("G", 1), ("H", 1), ("G", 0), ("H", 0), ("R1", 3)] + far + [("R0", 3)]
    return [("G", 2), ("H", 2)] + rest


def item_at(u, n):
    s = 1 if n >= FIRST[1] else 0
    items = item_list(s, u)
    n -= FIRST[s]
    return (s, *items[n]) if n < len(items) else (s, "", 0)


X_SENDS = {
    1: ("G", 0, 1), 2: ("F", 0, 2), 3: ("G", 0, 2), 4: ("F", 0, 1), 5: ("F", 0, 0), 7: ("F", 1, 3), 8: ("R", 0, 0),
    9: ("F", 1, 2), 10: ("G", 1, 1), 11: ("F", 1, 1), 12: ("G", 1, 2), 13: ("F", 1, 0), 14: ("G", 1, 3), 16: ("R", 1, 0),
}
X_TAKES = {2: (0, 0), 3: (0, 1), 5: (0, 2), 9: (1, 0), 12: (1, 1), 14: (1, 2), 16: (1, 3)}


def order_static(z):
    return ([0, 1, 2, 3], [1, 0, 2, 3], [2, 3, 1, 0], [3, 2, 1, 0])[z]


def fused_kernel(names, width, anc_ref, fac_ref, win_ref, piv_ref, str_ref, cols_hbm, out_hbm, *scratch):
    m = dict(zip(names, scratch, strict=True))
    cols_ref, out_ref = m["cols"], m["out"]
    fac, a_buf, win_st, piv_st = m["fac"], m["a_buf"], m["win"], m["piv"]
    lr_hi, lr_lo, lt_hi, lt_lo = m["lr_hi"], m["lr_lo"], m["lt_hi"], m["lt_lo"]
    tr_hi, tr_lo = m["tr_hi"], m["tr_lo"]
    own, near, y_own, y_near = m["own"], m["near"], m["y_own"], m["y_near"]
    p0, m0i, x0i, z0i = m["p0"], m["m0i"], m["x0i"], m["z0i"]
    p1, m1i, x1i, z1i = m["p1"], m["m1i"], m["x1i"], m["z1i"]

    me = lax.axis_index("pcol")
    core = lax.rem(me, 2)
    x = lax.rem(me // 2, 2)
    z = me // 4
    lane = me // 2
    rows = fac.shape[0]
    tile = width // 2
    mate = me + 1 - 2 * core

    def index(zz, xx, cc):
        return (zz * 2 + xx) * 2 + cc

    x_other = 1 - x
    across = index(z, x_other, core)

    def order(t):
        inner = (0, 0, 2, 3) if t else (1, 1, 1, 1)
        lowmid = inner[t] if t else 1
        highmid = 3 - lowmid
        return jnp.where(z == 0, t, jnp.where(z == 1, lowmid, jnp.where(z == 2, highmid, 3 - t)))

    def job_chip(q):
        return order(3 - q // 2) * 2 + (1 - x if q % 2 == 0 else x)

    def load_anc(q):
        at = pl.ds(pl.multiple_of(job_chip(q) * 2 * rows, 2 * rows), 2 * rows)
        return pltpu.make_async_copy(anc_ref.at[at, :], a_buf.at[q % 4], m["load_sem"].at[q])

    load_fac = pltpu.make_async_copy(fac_ref, fac, m["load_sem"].at[8])
    load_piv = pltpu.make_async_copy(piv_ref, piv_st, m["load_sem"].at[9])
    win_pairs = [(2, 1), (1, 0), (2, 0)]

    def load_win(n):
        j, k = win_pairs[n]
        block = win_ref.at[pl.ds(j * width, width), pl.ds(k * width, width)]
        return pltpu.make_async_copy(block, win_st.at[n], m["load_sem"].at[10 + n])

    load_fac.start()
    for q in range(4):
        load_anc(q).start()

    barrier = pltpu.get_barrier_semaphore()
    for d in range(1, LANES):
        peer = lax.rem(lane + d, LANES) * 2 + core
        pl.semaphore_signal(barrier, inc=1, device_id={"pcol": peer}, device_id_type=MESH)
    pl.semaphore_signal(barrier, inc=1, device_id={"pcol": mate}, device_id_type=MESH)

    common = []
    by_z = [[] for _ in range(Z)]
    log = [common]

    def go(make):
        make().start()
        log[0].append(make)

    def remote(src, dst, ssem, rsem, dest):
        return pltpu.make_async_remote_copy(
            src_ref=src, dst_ref=dst, send_sem=ssem, recv_sem=rsem, device_id={"pcol": dest}, device_id_type=MESH
        )

    def arrive(dst, rsem):
        remote(dst, dst, rsem, rsem, mate).wait_recv()

    def core_rows(c):
        return pl.ds(pl.multiple_of(c * rows, rows), rows)

    def own_at(s, zz, xx, c):
        return own.at[s, zz * 2 + xx, core_rows(c), :]

    def near_at(s, zz, c):
        return near.at[s, zz, core_rows(c), :]

    def own_send(s, zz, xx, kind, dest):
        def make():
            ref = own_at(s, zz, xx, core)
            return remote(ref, ref, m["own_s"].at[s, kind, zz * 2 + xx], m["own_r"].at[s, zz * 2 + xx, core], dest)
        go(make)

    def near_send(s, zz, kind, dest):
        def make():
            ref = near_at(s, zz, core)
            return remote(ref, ref, m["near_s"].at[s, kind, zz], m["near_r"].at[s, zz, core], dest)
        go(make)

    def own_wait(s, zz, xx, c):
        arrive(own_at(s, zz, xx, c), m["own_r"].at[s, zz * 2 + xx, c])

    def near_wait(s, zz, c):
        arrive(near_at(s, zz, c), m["near_r"].at[s, zz, c])

    def columns(t):
        return slice(t * tile, (t + 1) * tile)

    def mask(t):
        for piece in range(rows // tile):
            block = (me * (rows // tile) + piece) // 2
            kept = str_ref[t // 2, block].astype(jnp.float32)
            at = slice(piece * tile, (piece + 1) * tile)
            fac[at, columns(t)] = fac[at, columns(t)] * kept

    own_tiles, near_tiles, sum_tiles = (5, 2), (4, 1), (3, 0)

    load_fac.wait()
    mask(own_tiles[0])
    own[0, lane, core_rows(core), :] = fac[:, columns(own_tiles[0])]
    pl.semaphore_wait(barrier, LANES)

    def in_direction(direction, zz):
        return zz if direction == UP else Z - 1 - zz

    z_dests = (me + 4, me - 4)

    def z_dest(direction):
        return z_dests[direction]

    def landing(direction, zz, dest_z):
        return Z if direction == DOWN and dest_z == zz else dest_z

    def z_send(direction, zz, n):
        s, kind, v = item_at(in_direction(direction, zz), n)
        vz = in_direction(direction, v)
        first = in_direction(direction, zz) == 0
        dest = z_dest(direction)
        there = zz + 1 if direction == UP else zz - 1
        if kind == "G":
            own_send(s, vz, x, direction, dest)
        elif kind == "H":
            near_send(s, vz, direction, dest)
        elif kind == "X":
            own_send(s, vz, x_other, direction, dest)
        elif kind == "R1":
            arrive(m1i.at[s, vz], m["m1_r"].at[s, vz])
            value = p1[s, 0, vz] + m1i[s, vz]
            if not first:
                value = value + z1i[s, vz]
            p1[s, 0, vz] = value
            at = landing(direction, there, vz)
            go(lambda: remote(p1.at[s, 0, vz], z1i.at[s, at], m["z1_s"].at[s, vz], m["z1_r"].at[s, at], z_dest(direction)))
        elif kind == "R0":
            arrive(m0i.at[s, 0, vz], m["m0_r"].at[s, 0, vz])
            arrive(x0i.at[s, vz], m["x0_r"].at[s, vz])
            value = p0[s, 0, 0, vz] + m0i[s, 0, vz] + x0i[s, vz]
            if not first:
                value = value + z0i[s, vz]
            p0[s, 0, 0, vz] = value
            at = landing(direction, there, vz)
            go(lambda: remote(p0.at[s, 0, 0, vz], z0i.at[s, at], m["z0_s"].at[s, vz], m["z0_r"].at[s, at], z_dest(direction)))

    def z_arrival(direction, zz, n):
        u = in_direction(direction, zz)
        s, kind, v = item_at(u - 1, n)
        vz = in_direction(direction, v)
        if kind == "G":
            own_wait(s, vz, x, core)
            own_send(s, vz, x, MATE, mate)
        elif kind == "H":
            near_wait(s, vz, core)
            near_send(s, vz, MATE - 1, mate)
        elif kind == "X":
            own_wait(s, vz, x_other, core)
            own_send(s, vz, x_other, MATE, mate)
        elif kind == "R1":
            at = landing(direction, zz, vz)
            arrive(z1i.at[s, at], m["z1_r"].at[s, at])
        elif kind == "R0":
            at = landing(direction, zz, vz)
            arrive(z0i.at[s, at], m["z0_r"].at[s, at])

    def x_sum(s, v):
        arrive(m0i.at[s, 1, v], m["m0_r"].at[s, 1, v])
        p0[s, 0, 1, v] = p0[s, 0, 1, v] + m0i[s, 1, v]
        go(lambda: remote(p0.at[s, 0, 1, v], x0i.at[s, v], m["x0_s"].at[s, v], m["x0_r"].at[s, v], across))

    def x_near(s, zz):
        arrive(m1i.at[s, zz], m["m1_r"].at[s, zz])
        value = p1[s, 0, zz] + m1i[s, zz]
        if zz > 0:
            value = value + z1i[s, zz]
        if zz < Z - 1:
            value = value + z1i[s, Z]
        p1[s, 0, zz] = value
        go(lambda: remote(p1.at[s, 0, zz], x1i.at[s], m["x1_s"].at[s], m["x1_r"].at[s], across))

    def x_step(kind, s, t, zz):
        v = order_static(zz)[t]
        if kind == "G":
            own_send(s, v, x, ACROSS, across)
        elif kind == "F":
            x_sum(s, v)
        else:
            x_near(s, zz)

    def x_arrival(s, t, zz):
        v = order_static(zz)[t]
        own_wait(s, v, x_other, core)
        own_send(s, v, x_other, MATE, mate)

    def events(step):
        for zz in range(Z):
            log[0] = by_z[zz]

            @pl.when(z == zz)
            def _():
                for direction in (UP, DOWN):
                    if in_direction(direction, zz) > 0 and 0 <= step - 1 < TOTAL:
                        z_arrival(direction, zz, step - 1)
                for direction in (UP, DOWN):
                    if in_direction(direction, zz) < Z - 1 and 2 <= step + 1 < TOTAL:
                        z_send(direction, zz, step + 1)
                if step in X_SENDS:
                    x_step(*X_SENDS[step], zz)
                if step in X_TAKES:
                    x_arrival(*X_TAKES[step], zz)

            log[0] = common

    def begin(s):
        own_send(s, z, x, ACROSS, across)
        own_send(s, z, x, MATE, mate)
        near_send(s, z, MATE - 1, mate)

    for zz in range(Z):
        log[0] = by_z[zz]

        @pl.when(z == zz)
        def _():
            for direction in (UP, DOWN):
                if in_direction(direction, zz) < Z - 1:
                    z_send(direction, zz, 0)

        log[0] = common
    own_send(0, z, x, ACROSS, across)
    own_send(0, z, x, MATE, mate)

    mask(near_tiles[0])
    near[0, z, core_rows(core), :] = fac[:, columns(near_tiles[0])]
    near_send(0, z, MATE - 1, mate)
    for zz in range(Z):
        log[0] = by_z[zz]

        @pl.when(z == zz)
        def _():
            for direction in (UP, DOWN):
                if in_direction(direction, zz) < Z - 1:
                    z_send(direction, zz, 1)

        log[0] = common

    for t in (sum_tiles[0], sum_tiles[1], near_tiles[1], own_tiles[1]):
        mask(t)
    for n, t in enumerate((sum_tiles[0], sum_tiles[1], near_tiles[0], near_tiles[1])):
        high, low = split(fac[:, columns(t)])
        lr_hi[:, columns(n)] = high
        lr_lo[:, columns(n)] = low

    def chip_job(q):
        v = order(3 - q // 2)
        other = q % 2 == 0
        side = 1 if other else 0
        chip = job_chip(q)
        load_anc(q).wait()

        def both(i, carry):
            c = core + (1 - 2 * core) * (1 - i)
            pair = split(a_buf[q % 4, core_rows(c), :])
            count = (4 if other else 2) * tile
            value = dot3(pair, (lr_hi[:, :count], lr_lo[:, :count]))
            for s in range(STAGES):
                p0[s, 1 - i, side, v] = value[:, columns(s)]
                if other:
                    p1[s, 1 - i, v] = value[:, columns(2 + s)]
            return carry

        lax.fori_loop(0, 2, both, 0)
        for s in range(STAGES):
            go(lambda s=s: remote(p0.at[s, 1, side, v], m0i.at[s, side, v], m["m0_s"].at[s, side, v], m["m0_r"].at[s, side, v], mate))
            if other:
                go(lambda s=s: remote(p1.at[s, 1, v], m1i.at[s, v], m["m1_s"].at[s, v], m["m1_r"].at[s, v], mate))

        def flip(c, carry):
            high, low = split(a_buf[q % 4, core_rows(c), :].T)
            at = pl.ds(pl.multiple_of(c * rows, rows), rows)
            tr_hi[chip, :, at] = high
            tr_lo[chip, :, at] = low
            return carry

        lax.fori_loop(0, 2, flip, 0)
        if q + 4 < 8:
            load_anc(q + 4).start()

    def pair_job(block, total, chip, first):
        high, low = split(block)
        left, rest = tr_hi[chip], tr_lo[chip]
        wide = jnp.dot(left, jnp.concatenate([high, low], axis=1), preferred_element_type=jnp.float32)
        value = wide[:, :tile] + (wide[:, tile:] + jnp.dot(rest, high, preferred_element_type=jnp.float32))
        if first:
            total[...] = value
        else:
            total[...] += value

    def own_job(s, t, other):
        zz = order(t)
        xx = 1 - x if other else x
        own_wait(s, zz, xx, 1 - core)
        pair_job(own[s, zz * 2 + xx], y_own.at[s], zz * 2 + xx, t == 0 and not other)

    def near_job(s, t):
        zz = order(t)
        near_wait(s, zz, 1 - core)
        pair_job(near[s, zz], y_near.at[s], zz * 2 + x, t == 0)

    def finish_own(s):
        cols_ref[:, columns(own_tiles[s])] = y_own[s]

    def finish(s):
        arrive(x1i.at[s], m["x1_r"].at[s])
        cols_ref[:, columns(near_tiles[s])] = y_near[s] + x1i[s]
        arrive(m0i.at[s, 0, z], m["m0_r"].at[s, 0, z])
        arrive(x0i.at[s, z], m["x0_r"].at[s, z])
        value = p0[s, 0, 0, z] + m0i[s, 0, z] + x0i[s, z]
        low = z0i[s, z]
        high = z0i[s, Z]
        value = value + jnp.where(z > 0, low, 0.0) + jnp.where(z < Z - 1, high, 0.0)
        cols_ref[:, columns(sum_tiles[s])] = value

    half_cols = 3 * tile
    sum_list = (
        [(q, p) for q in (3, 4, 5) for p in range(q + 1)],
        [(2, p) for p in range(3)],
        [(q, p) for q in (0, 1) for p in range(q + 1)],
    )

    def inner_early():
        flipped = split(cols_ref[:, half_cols:].T)
        value = dot3(flipped, split(fac[...]))
        for n, (q, p) in enumerate(sum_list[0]):
            m["part0"][n] = value[(q - 3) * tile : (q - 2) * tile, columns(p)]

    def inner_middle():
        value = dot3(split(cols_ref[:, columns(2)].T), split(fac[:, :half_cols]))
        for n, (q, p) in enumerate(sum_list[1]):
            m["part1"][n] = value[:, columns(p)]

    def inner_late():
        value = dot3((lt_hi[:width, :], lt_lo[:width, :]), split(cols_ref[:, :width]))
        for n, (q, p) in enumerate(sum_list[2]):
            m["part2"][n] = value[columns(q), columns(p)]

    groups = {
        "mate": (2, core, lambda n: index(z, x, n)),
        "x": (2, x, lambda n: index(z, n, core)),
        "z": (Z, z, lambda n: index(n, x, core)),
        "lane": (LANES, lane, lambda n: n * 2 + core),
    }

    def reducer(s):
        plan = LEVELS[s]
        sums = m[f"sum{s}"]
        sizes = [tile]
        for name in plan:
            sizes.append(sizes[-1] // groups[name][0])
        base = [0]
        for name, size in zip(plan, sizes[1:]):
            base.append(base[-1] + groups[name][1] * size)

        def held(level):
            return m[f"part{s}"] if level == 0 else m[f"held{s}_{level}"]

        def peer_of(level, d):
            count, mine, _ = groups[plan[level]]
            return 1 - mine if count == 2 else lax.rem(mine + d, count)

        def send_down(level):
            count, mine, device = groups[plan[level]]
            size = sizes[level + 1]
            for d in range(1, count):
                def make(d=d):
                    peer = peer_of(level, d)
                    src = held(level).at[:, pl.ds(pl.multiple_of(peer * size, size), size), :]
                    return remote(
                        src, m[f"slot{s}_{level}"].at[mine], m[f"ds{s}"].at[level, peer], m[f"dr{s}"].at[level, mine], device(peer)
                    )
                go(make)

        def take_down(level):
            count, mine, device = groups[plan[level]]
            size = sizes[level + 1]
            slot = m[f"slot{s}_{level}"]
            total = held(level)[:, pl.ds(pl.multiple_of(mine * size, size), size), :]
            for d in range(1, count):
                peer = peer_of(level, d)
                arrive(slot.at[peer], m[f"dr{s}"].at[level, peer])
                total = total + slot[peer]
            if level + 1 < len(plan):
                held(level + 1)[...] = total
            else:
                sums[:, pl.ds(pl.multiple_of(base[-1], size), size), :] = total

        def part_at(level, owner):
            size = sizes[level + 1]
            return sums.at[:, pl.ds(pl.multiple_of(base[level] + owner * size, size), size), :]

        def send_up(level):
            count, mine, device = groups[plan[level]]
            for d in range(1, count):
                def make(d=d):
                    peer = peer_of(level, d)
                    ref = part_at(level, mine)
                    return remote(ref, ref, m[f"us{s}"].at[level, peer], m[f"ur{s}"].at[level, mine], device(peer))
                go(make)

        def take_up(level):
            count, mine, device = groups[plan[level]]
            for d in range(1, count):
                peer = peer_of(level, d)
                arrive(part_at(level, peer), m[f"ur{s}"].at[level, peer])

        steps = [lambda: send_down(0)]
        for level in range(len(plan)):
            def step(level=level):
                take_down(level)
                if level + 1 < len(plan):
                    send_down(level + 1)
                else:
                    send_up(level)
            steps.append(step)
        for level in range(len(plan) - 1, -1, -1):
            def step(level=level):
                take_up(level)
                if level > 0:
                    send_up(level - 1)
            steps.append(step)
        return steps

    inner = m["inner"]
    blocks = [(2, 2), (2, 1), (2, 0), (1, 1), (1, 0), (0, 0)]

    def place(s):
        for n, (q, p) in enumerate(sum_list[s]):
            value = m[f"sum{s}"][n]
            at = blocks.index((q // 2, p // 2))
            inner[at, (q % 2) * tile : (q % 2 + 1) * tile, (p % 2) * tile : (p % 2 + 1) * tile] = value
            if q // 2 == p // 2 and q != p:
                inner[at, (p % 2) * tile : (p % 2 + 1) * tile, (q % 2) * tile : (q % 2 + 1) * tile] = value.T

    def n_block(j, k):
        return inner[blocks.index((j, k))]

    def fac_block(j, k):
        return win_st[win_pairs.index((j, k))]

    def save_block(j, k):
        block = out_ref.at[pl.ds(j * width, width), pl.ds(k * width, width)]
        target = out_hbm.at[pl.ds(j * width, width), pl.ds(k * width, width)]
        return pltpu.make_async_copy(block, target, m["save_sem"].at[j, k])

    def save_column(k):
        at = pl.ds(k * width, width)
        return pltpu.make_async_copy(cols_ref.at[:, at], cols_hbm.at[:, at], m["save_sem"].at[3, k])

    def put(j, k, value):
        out_ref[j * width : (j + 1) * width, k * width : (k + 1) * width] = value
        save_block(j, k).start()

    def got(j, k):
        return out_ref[j * width : (j + 1) * width, k * width : (k + 1) * width]

    early = m["early"]

    def window_first():
        put(2, 2, piv_st[2] + n_block(2, 2))
        value = n_block(2, 1) - mul(got(2, 2), fac_block(2, 1))
        put(2, 1, value)
        put(1, 2, value.T)
        value = n_block(2, 0) - mul(got(2, 1), fac_block(1, 0)) - mul(got(2, 2), fac_block(2, 0))
        put(2, 0, value)
        put(0, 2, value.T)

    def window_second():
        flip21 = split(fac_block(2, 1).T)
        known = piv_st[1] - mul(n_block(2, 1).T, fac_block(2, 1)) - dot3(flip21, split(got(2, 1)))
        early[0] = known
        turned = dot3(flip21, split(n_block(2, 0)))
        left = jnp.concatenate([fac_block(2, 1).T, known, got(1, 2)], axis=1)
        right = jnp.concatenate([n_block(2, 0), fac_block(1, 0), fac_block(2, 0)], axis=0)
        early[1] = mul(left, right)
        early[2] = (
            piv_st[0]
            + mul(turned.T, fac_block(1, 0))
            - mul(n_block(2, 0).T, fac_block(2, 0))
            - mul(fac_block(2, 0).T, got(2, 0))
        )

    def window_last():
        put(1, 1, early[0] + n_block(1, 1))
        value = n_block(1, 0) - early[1] - mul(n_block(1, 1), fac_block(1, 0))
        put(1, 0, value)
        put(0, 1, value.T)
        put(0, 0, early[2] + n_block(0, 0) - mul(n_block(1, 0).T, fac_block(1, 0)) - mul(fac_block(1, 0).T, value))

    def column(k):
        return cols_ref[:, k * width : (k + 1) * width]

    def put_column(k):
        value = column(k)
        for j in range(k + 1, 3):
            value = value + mul(column(j), fac_block(j, k))
        cols_ref[:, k * width : (k + 1) * width] = -value

    chip_job(0)
    chip_job(1)
    x_sum(0, order(3))
    load_piv.start()
    for n in range(3):
        load_win(n).start()
    events(1)
    chip_job(2)
    chip_job(3)
    events(2)
    chip_job(4)
    chip_job(5)
    own[1, lane, core_rows(core), :] = fac[:, columns(own_tiles[1])]
    near[1, z, core_rows(core), :] = fac[:, columns(near_tiles[1])]
    events(3)
    chip_job(6)
    chip_job(7)
    events(4)
    own_job(0, 0, False)
    own_job(0, 1, False)
    events(5)
    near_job(0, 0)
    near_job(0, 1)
    own_job(0, 0, True)
    own_job(0, 1, True)
    events(6)
    begin(1)
    own_job(0, 2, False)
    near_job(0, 2)
    own_job(0, 2, True)
    events(7)
    own_job(0, 3, False)
    high, low = split(fac[:, :half_cols].T)
    lt_hi[...] = high
    lt_lo[...] = low
    events(8)
    near_job(0, 3)
    events(9)
    own_job(0, 3, True)
    events(10)
    finish_own(0)
    finish(0)
    inner_early()
    cols_ref[:, 2 * width :] = -cols_ref[:, 2 * width :]
    save_column(2).start()
    first, middle, last = reducer(0), reducer(1), reducer(2)
    first[0]()
    own_job(1, 0, False)
    first[1]()
    events(11)
    own_job(1, 1, False)
    near_job(1, 0)
    near_job(1, 1)
    own_job(1, 0, True)
    events(12)
    first[2]()
    events(13)
    own_job(1, 1, True)
    own_job(1, 2, False)
    near_job(1, 2)
    events(14)
    first[3]()
    own_job(1, 2, True)
    load_piv.wait()
    for n in range(3):
        load_win(n).wait()
    events(15)
    own_job(1, 3, False)
    events(16)
    near_job(1, 3)
    own_job(1, 3, True)
    finish_own(1)
    inner_middle()
    middle[0]()
    middle[1]()
    events(17)
    finish(1)
    inner_late()
    last[0]()
    first[4]()
    middle[2]()
    put_column(1)
    save_column(1).start()
    last[1]()
    put_column(0)
    save_column(0).start()
    first[5]()
    middle[3]()
    last[2]()
    first[6]()
    place(0)
    window_first()
    middle[4]()
    window_second()
    for step in last[3:]:
        step()
    place(1)
    place(2)
    window_last()
    for k in range(3):
        save_column(k).wait()
        for j in range(3):
            save_block(j, k).wait()

    for make in common:
        make().wait_send()
    for zz in range(Z):

        @pl.when(z == zz)
        def _():
            for make in by_z[zz]:
                make().wait_send()


LEVELS = (("mate", "x", "z"), ("mate", "lane"), ("mate", "lane"))
COUNT = dict(mate=2, x=2, z=Z, lane=LANES)


def fused(anc_inverse, anc_factor, win_factor, pivot_inverse, structure):
    steps, width = pivot_inverse.shape[:2]
    rows, all_cols = anc_factor.shape
    tile = width // 2
    f32, b16 = jnp.float32, jnp.bfloat16
    dma = pltpu.SemaphoreType.DMA
    block = (rows, tile)
    pair = (2 * rows, tile)
    spaces = dict(
        cols=pltpu.VMEM((rows, all_cols), f32),
        out=pltpu.VMEM((all_cols, all_cols), f32),
        save_sem=dma((4, 3)),
        fac=pltpu.VMEM((rows, all_cols), f32),
        a_buf=pltpu.VMEM((4, 2 * rows, rows), f32),
        win=pltpu.VMEM((3, width, width), f32),
        piv=pltpu.VMEM(pivot_inverse.shape, f32),
        lr_hi=pltpu.VMEM((rows, 4 * tile), b16),
        lr_lo=pltpu.VMEM((rows, 4 * tile), b16),
        lt_hi=pltpu.VMEM((3 * tile, rows), b16),
        lt_lo=pltpu.VMEM((3 * tile, rows), b16),
        tr_hi=pltpu.VMEM((LANES, rows, 2 * rows), b16),
        tr_lo=pltpu.VMEM((LANES, rows, 2 * rows), b16),
        own=pltpu.VMEM((STAGES, LANES, *pair), f32),
        near=pltpu.VMEM((STAGES, Z, *pair), f32),
        y_own=pltpu.VMEM((STAGES, *block), f32),
        y_near=pltpu.VMEM((STAGES, *block), f32),
        p0=pltpu.VMEM((STAGES, 2, 2, Z, *block), f32),
        m0i=pltpu.VMEM((STAGES, 2, Z, *block), f32),
        x0i=pltpu.VMEM((STAGES, Z, *block), f32),
        z0i=pltpu.VMEM((STAGES, Z + 1, *block), f32),
        p1=pltpu.VMEM((STAGES, 2, Z, *block), f32),
        m1i=pltpu.VMEM((STAGES, Z, *block), f32),
        x1i=pltpu.VMEM((STAGES, *block), f32),
        z1i=pltpu.VMEM((STAGES, Z + 1, *block), f32),
        inner=pltpu.VMEM((6, width, width), f32),
        early=pltpu.VMEM((3, width, width), f32),
        load_sem=dma((13,)),
        own_s=dma((STAGES, 4, LANES)),
        own_r=dma((STAGES, LANES, 2)),
        near_s=dma((STAGES, 3, Z)),
        near_r=dma((STAGES, Z, 2)),
        m0_s=dma((STAGES, 2, Z)),
        m0_r=dma((STAGES, 2, Z)),
        x0_s=dma((STAGES, Z)),
        x0_r=dma((STAGES, Z)),
        z0_s=dma((STAGES, Z)),
        z0_r=dma((STAGES, Z + 1)),
        m1_s=dma((STAGES, Z)),
        m1_r=dma((STAGES, Z)),
        x1_s=dma((STAGES,)),
        x1_r=dma((STAGES,)),
        z1_s=dma((STAGES, Z)),
        z1_r=dma((STAGES, Z + 1)),
    )
    for s, plan in enumerate(LEVELS):
        tiles = (15, 3, 3)[s]
        size = tile
        spaces[f"part{s}"] = pltpu.VMEM((tiles, tile, tile), f32)
        spaces[f"sum{s}"] = pltpu.VMEM((tiles, tile, tile), f32)
        for level, name in enumerate(plan):
            size //= COUNT[name]
            spaces[f"slot{s}_{level}"] = pltpu.VMEM((COUNT[name], tiles, size, tile), f32)
            if level + 1 < len(plan):
                spaces[f"held{s}_{level + 1}"] = pltpu.VMEM((tiles, size, tile), f32)
        for kind in ("ds", "dr", "us", "ur"):
            spaces[f"{kind}{s}"] = dma((len(plan), LANES))
    whole = pl.BlockSpec(memory_space=pl.ANY)
    return pl.pallas_call(
        functools.partial(fused_kernel, tuple(spaces), width),
        out_shape=(
            jax.ShapeDtypeStruct((rows, all_cols), f32),
            jax.ShapeDtypeStruct((all_cols, all_cols), f32),
        ),
        in_specs=[whole, whole, whole, whole, pl.BlockSpec(memory_space=pltpu.SMEM)],
        out_specs=(whole, whole),
        scratch_shapes=list(spaces.values()),
        compiler_params=pltpu.CompilerParams(
            collective_id=0, has_side_effects=True, vmem_limit_bytes=63 * 2**20
        ),
    )(anc_inverse, anc_factor, win_factor, pivot_inverse, structure)


def land_kernel(parts, *refs):
    count = len(parts)
    sources, targets = refs[:count], refs[count : 2 * count]
    held, sem = refs[2 * count : 3 * count], refs[3 * count]
    copies = []
    for n, pieces in enumerate(parts):
        size = sources[n].shape[0] // pieces
        for i in range(pieces):
            at = pl.ds(i * size, size)
            read = pltpu.make_async_copy(sources[n].at[at, :], held[n].at[at, :], sem.at[0, len(copies)])
            write = pltpu.make_async_copy(held[n].at[at, :], targets[n].at[at, :], sem.at[1, len(copies)])
            read.start()
            copies.append((read, write))
    for read, write in copies:
        read.wait()
        write.start()
    for read, write in copies:
        write.wait()


def land(*arrays):
    whole = pl.BlockSpec(memory_space=pl.ANY)
    parts = (3, 6)
    return pl.pallas_call(
        functools.partial(land_kernel, parts),
        out_shape=tuple(jax.ShapeDtypeStruct(a.shape, a.dtype) for a in arrays),
        in_specs=[whole] * len(arrays),
        out_specs=(whole,) * len(arrays),
        scratch_shapes=[pltpu.VMEM(a.shape, a.dtype) for a in arrays] + [pltpu.SemaphoreType.DMA((2, sum(parts)))],
    )(*arrays)


precise = lax.Precision.HIGHEST


def product(left, right):
    return jnp.dot(left, right, precision=precise, preferred_element_type=jnp.float32)


def on_device(anc_inverse, anc_factor, win_factor, pivot_inverse, structure):
    row_count = lax.axis_size("prow")
    col_count = lax.axis_size("pcol")
    steps, width = pivot_inverse.shape[:2]
    fits = steps == 3 and 2 * anc_factor.shape[0] == 3 * width and width % 256 == 0
    if row_count == 1 and col_count == 4 * Z and fits:
        return land(*fused(anc_inverse, anc_factor, win_factor, pivot_inverse, structure))
    row_index = lax.axis_index("prow")
    col_index = lax.axis_index("pcol")
    block_rows = anc_inverse.shape[0]
    block_cols = anc_inverse.shape[1]
    steps_total = pivot_inverse.shape[0]
    width = pivot_inverse.shape[1]
    all_cols = anc_factor.shape[1]
    block_count = structure.shape[1]
    ratio_cols = col_count // row_count
    share_rows = block_rows // col_count
    structure_cols = structure.T.astype(jnp.float32)
    global_rows = col_index * block_cols + lax.iota(jnp.int32, block_cols)
    onehot_rows = (
        (global_rows // width)[:, None] == lax.iota(jnp.int32, block_count)[None, :]
    ).astype(jnp.float32)
    kept_rows = product(onehot_rows, structure_cols)
    share_offset = col_index * share_rows
    share_global = (row_index * col_count + col_index) * share_rows + lax.iota(
        jnp.int32, share_rows
    )
    onehot_share = (
        (share_global // width)[:, None] == lax.iota(jnp.int32, block_count)[None, :]
    ).astype(jnp.float32)
    kept_share = product(onehot_share, structure_cols)
    slot_ids = lax.iota(jnp.int32, col_count)
    source_flag = (slot_ids // row_count == col_index - row_index * ratio_cols).astype(jnp.float32)
    pieces = jnp.tile(anc_factor.reshape(row_count, share_rows, all_cols), (ratio_cols, 1, 1))
    outgoing = pieces * source_flag[:, None, None]
    incoming = lax.all_to_all(outgoing, "pcol", split_axis=0, concat_axis=0, tiled=True)
    factor_share = jnp.sum(incoming, axis=0)
    column_store = {}
    share_store = {}
    window_blocks = {}
    for k in range(steps_total - 1, -1, -1):
        first_col = k * width
        factor_now = anc_factor[:, first_col : first_col + width] * kept_rows[:, k : k + 1]
        share_factor = factor_share[:, first_col : first_col + width] * kept_share[:, k : k + 1]
        finished = list(range(k + 1, steps_total))
        if finished:
            stacked = jnp.concatenate([column_store[j] for j in finished], axis=1)
            factor_win = win_factor[first_col + width :, first_col : first_col + width]

        def term_rows(start, count, factor_now=factor_now):
            return product(anc_inverse, factor_now)

        share_image = lax.psum_scatter(
            term_rows(jnp.int32(0), share_rows * lax.axis_size("pcol")),
            "pcol",
            scatter_dimension=0,
            tiled=True,
        )
        if finished:
            share_image = share_image + product(
                lax.dynamic_slice_in_dim(stacked, share_offset, share_rows, 0), factor_win
            )
        share_column = -share_image
        column_now = lax.all_gather(share_column, "pcol", axis=0, tiled=True)
        crossings = [product(share_store[j].T, share_factor) for j in finished]
        pivot_part = product(share_factor.T, share_column)
        cross_sums = []
        if finished:
            cross_total = lax.psum(jnp.stack(crossings), ("prow", "pcol"))
            cross_sums = [cross_total[position] for position in range(len(finished))]
        pivot_sum = lax.psum(pivot_part, ("prow", "pcol"))
        for position, j in enumerate(finished):
            running = cross_sums[position]
            for i in finished:
                running = running + product(
                    window_blocks[j, i],
                    win_factor[i * width : (i + 1) * width, first_col : first_col + width],
                )
            window_blocks[j, k] = -running
            window_blocks[k, j] = -running.T
        pivot_block = pivot_inverse[k] - pivot_sum
        for j in finished:
            pivot_block = pivot_block - product(
                win_factor[j * width : (j + 1) * width, first_col : first_col + width].T,
                window_blocks[j, k],
            )
        window_blocks[k, k] = pivot_block
        column_store[k] = column_now
        share_store[k] = share_column
    anc_columns = jnp.concatenate([share_store[k] for k in range(steps_total)], axis=1)
    win_inverse = jnp.concatenate(
        [
            jnp.concatenate([window_blocks[i, k] for k in range(steps_total)], axis=1)
            for i in range(steps_total)
        ],
        axis=0,
    )
    return (anc_columns, win_inverse)


def solution(mesh):
    in_specs = (
        P(("pole", "prow"), "pcol"),
        P(("pole", "pcol"), None),
        P("pole", None),
        P("pole", None, None),
        P(),
    )
    out_specs = (P(("pole", "prow", "pcol"), None), P("pole", None))
    return jax.shard_map(
        on_device, mesh=mesh, in_specs=in_specs, out_specs=out_specs, check_vma=False
    )
```

```python
import functools

import jax
import jax.numpy as jnp
from jax import lax
from jax.experimental import pallas as pl
from jax.experimental.pallas import tpu as pltpu
from jax.sharding import PartitionSpec as P

MESH = pl.DeviceIdType.MESH
UP, DOWN, ACROSS, MATE = range(4)
Z = 4
LANES = 8


def split(value):
    high = value.astype(jnp.bfloat16)
    low = (value - high.astype(jnp.float32)).astype(jnp.bfloat16)
    return high, low


def dot3(left, right):
    (lh, ll), (rh, rl) = left, right
    dot = functools.partial(jnp.dot, preferred_element_type=jnp.float32)
    return dot(lh, rh) + (dot(lh, rl) + dot(ll, rh))


def mul(left, right):
    return dot3(split(left), split(right))


STAGES = 2
FIRST = (0, 8)
TOTAL = 16


def item_list(s, u):
    if u == 0:
        rest = [("R1", 3), ("R0", 3), ("R1", 2), ("R0", 2), ("R1", 1), ("R0", 1)]
        return [("G", 0), ("H", 0)] + rest
    far = []
    if u == 1:
        rest = [("R1", 3)] + far + [("R0", 3), ("R1", 2), ("R0", 2)]
        return [("G", 1), ("H", 1), ("G", 0), ("H", 0)] + rest
    rest = [("G", 1), ("H", 1), ("G", 0), ("H", 0), ("R1", 3)] + far + [("R0", 3)]
    return [("G", 2), ("H", 2)] + rest


def item_at(u, n):
    s = 1 if n >= FIRST[1] else 0
    items = item_list(s, u)
    n -= FIRST[s]
    return (s, *items[n]) if n < len(items) else (s, "", 0)


X_SENDS = {
    1: ("G", 0, 1), 2: ("F", 0, 2), 3: ("G", 0, 2), 4: ("F", 0, 1), 5: ("G", 0, 3), 6: ("F", 0, 0), 7: ("R", 0, 0), 8: ("F", 1, 3),
    9: ("F", 1, 2), 10: ("G", 1, 1), 11: ("F", 1, 1), 12: ("G", 1, 2), 13: ("F", 1, 0), 14: ("G", 1, 3), 15: ("R", 1, 0),
}
X_TAKES = {2: (0, 0), 3: (0, 1), 5: (0, 2), 7: (0, 3), 9: (1, 0), 12: (1, 1), 14: (1, 2), 16: (1, 3)}


def order_static(z):
    return ([0, 1, 2, 3], [1, 0, 2, 3], [2, 3, 1, 0], [3, 2, 1, 0])[z]


def fused_kernel(names, width, anc_ref, fac_ref, win_ref, piv_ref, str_ref, cols_hbm, out_hbm, *scratch):
    m = dict(zip(names, scratch, strict=True))
    cols_ref, out_ref = m["cols"], m["out"]
    fac, a_buf, win_st, piv_st = m["fac"], m["a_buf"], m["win"], m["piv"]
    lr_hi, lr_lo, lt_hi, lt_lo = m["lr_hi"], m["lr_lo"], m["lt_hi"], m["lt_lo"]
    tr_hi, tr_lo = m["tr_hi"], m["tr_lo"]
    own, near, y_own, y_near = m["own"], m["near"], m["y_own"], m["y_near"]
    p0, m0i, x0i, z0i = m["p0"], m["m0i"], m["x0i"], m["z0i"]
    p1, m1i, x1i, z1i = m["p1"], m["m1i"], m["x1i"], m["z1i"]

    me = lax.axis_index("pcol")
    core = lax.rem(me, 2)
    x = lax.rem(me // 2, 2)
    z = me // 4
    lane = me // 2
    rows = fac.shape[0]
    tile = width // 2
    mate = me + 1 - 2 * core

    def index(zz, xx, cc):
        return (zz * 2 + xx) * 2 + cc

    x_other = 1 - x
    across = index(z, x_other, core)

    def order(t):
        inner = (0, 0, 2, 3) if t else (1, 1, 1, 1)
        lowmid = inner[t] if t else 1
        highmid = 3 - lowmid
        return jnp.where(z == 0, t, jnp.where(z == 1, lowmid, jnp.where(z == 2, highmid, 3 - t)))

    def job_chip(q):
        return order(3 - q // 2) * 2 + (1 - x if q % 2 == 0 else x)

    def load_anc(q):
        at = pl.ds(pl.multiple_of(job_chip(q) * 2 * rows, 2 * rows), 2 * rows)
        return pltpu.make_async_copy(anc_ref.at[at, :], a_buf.at[q % 4], m["load_sem"].at[q])

    load_fac = pltpu.make_async_copy(fac_ref, fac, m["load_sem"].at[8])
    load_piv = pltpu.make_async_copy(piv_ref, piv_st, m["load_sem"].at[9])
    win_pairs = [(2, 1), (1, 0), (2, 0)]

    def load_win(n):
        j, k = win_pairs[n]
        block = win_ref.at[pl.ds(j * width, width), pl.ds(k * width, width)]
        return pltpu.make_async_copy(block, win_st.at[n], m["load_sem"].at[10 + n])

    load_fac.start()
    for q in range(4):
        load_anc(q).start()

    barrier = pltpu.get_barrier_semaphore()
    for d in range(1, LANES):
        peer = lax.rem(lane + d, LANES) * 2 + core
        pl.semaphore_signal(barrier, inc=1, device_id={"pcol": peer}, device_id_type=MESH)
    pl.semaphore_signal(barrier, inc=1, device_id={"pcol": mate}, device_id_type=MESH)

    common = []
    by_z = [[] for _ in range(Z)]
    log = [common]

    def go(make):
        make().start()
        log[0].append(make)

    def remote(src, dst, ssem, rsem, dest):
        return pltpu.make_async_remote_copy(
            src_ref=src, dst_ref=dst, send_sem=ssem, recv_sem=rsem, device_id={"pcol": dest}, device_id_type=MESH
        )

    def arrive(dst, rsem):
        remote(dst, dst, rsem, rsem, mate).wait_recv()

    def core_rows(c):
        return pl.ds(pl.multiple_of(c * rows, rows), rows)

    def own_at(s, zz, xx, c):
        return own.at[s, zz * 2 + xx, core_rows(c), :]

    def near_at(s, zz, c):
        return near.at[s, zz, core_rows(c), :]

    def own_send(s, zz, xx, kind, dest):
        def make():
            ref = own_at(s, zz, xx, core)
            return remote(ref, ref, m["own_s"].at[s, kind, zz * 2 + xx], m["own_r"].at[s, zz * 2 + xx, core], dest)
        go(make)

    def near_send(s, zz, kind, dest):
        def make():
            ref = near_at(s, zz, core)
            return remote(ref, ref, m["near_s"].at[s, kind, zz], m["near_r"].at[s, zz, core], dest)
        go(make)

    def own_wait(s, zz, xx, c):
        arrive(own_at(s, zz, xx, c), m["own_r"].at[s, zz * 2 + xx, c])

    def near_wait(s, zz, c):
        arrive(near_at(s, zz, c), m["near_r"].at[s, zz, c])

    def columns(t):
        return slice(t * tile, (t + 1) * tile)

    def mask(t):
        for piece in range(rows // tile):
            block = (me * (rows // tile) + piece) // 2
            kept = str_ref[t // 2, block].astype(jnp.float32)
            at = slice(piece * tile, (piece + 1) * tile)
            fac[at, columns(t)] = fac[at, columns(t)] * kept

    own_tiles, near_tiles, sum_tiles = (5, 2), (4, 1), (3, 0)

    load_fac.wait()
    mask(own_tiles[0])
    own[0, lane, core_rows(core), :] = fac[:, columns(own_tiles[0])]
    pl.semaphore_wait(barrier, LANES)

    def in_direction(direction, zz):
        return zz if direction == UP else Z - 1 - zz

    z_dests = (me + 4, me - 4)

    def z_dest(direction):
        return z_dests[direction]

    def landing(direction, zz, dest_z):
        return Z if direction == DOWN and dest_z == zz else dest_z

    def z_send(direction, zz, n):
        s, kind, v = item_at(in_direction(direction, zz), n)
        vz = in_direction(direction, v)
        first = in_direction(direction, zz) == 0
        dest = z_dest(direction)
        there = zz + 1 if direction == UP else zz - 1
        if kind == "G":
            own_send(s, vz, x, direction, dest)
        elif kind == "H":
            near_send(s, vz, direction, dest)
        elif kind == "X":
            own_send(s, vz, x_other, direction, dest)
        elif kind == "R1":
            arrive(m1i.at[s, vz], m["m1_r"].at[s, vz])
            value = p1[s, 0, vz] + m1i[s, vz]
            if not first:
                value = value + z1i[s, vz]
            p1[s, 0, vz] = value
            at = landing(direction, there, vz)
            go(lambda: remote(p1.at[s, 0, vz], z1i.at[s, at], m["z1_s"].at[s, vz], m["z1_r"].at[s, at], z_dest(direction)))
        elif kind == "R0":
            arrive(m0i.at[s, 0, vz], m["m0_r"].at[s, 0, vz])
            arrive(x0i.at[s, vz], m["x0_r"].at[s, vz])
            value = p0[s, 0, 0, vz] + m0i[s, 0, vz] + x0i[s, vz]
            if not first:
                value = value + z0i[s, vz]
            p0[s, 0, 0, vz] = value
            at = landing(direction, there, vz)
            go(lambda: remote(p0.at[s, 0, 0, vz], z0i.at[s, at], m["z0_s"].at[s, vz], m["z0_r"].at[s, at], z_dest(direction)))

    def z_arrival(direction, zz, n):
        u = in_direction(direction, zz)
        s, kind, v = item_at(u - 1, n)
        vz = in_direction(direction, v)
        if kind == "G":
            own_wait(s, vz, x, core)
            own_send(s, vz, x, MATE, mate)
        elif kind == "H":
            near_wait(s, vz, core)
            near_send(s, vz, MATE - 1, mate)
        elif kind == "X":
            own_wait(s, vz, x_other, core)
            own_send(s, vz, x_other, MATE, mate)
        elif kind == "R1":
            at = landing(direction, zz, vz)
            arrive(z1i.at[s, at], m["z1_r"].at[s, at])
        elif kind == "R0":
            at = landing(direction, zz, vz)
            arrive(z0i.at[s, at], m["z0_r"].at[s, at])

    def x_sum(s, v):
        arrive(m0i.at[s, 1, v], m["m0_r"].at[s, 1, v])
        p0[s, 0, 1, v] = p0[s, 0, 1, v] + m0i[s, 1, v]
        go(lambda: remote(p0.at[s, 0, 1, v], x0i.at[s, v], m["x0_s"].at[s, v], m["x0_r"].at[s, v], across))

    def x_near(s, zz):
        arrive(m1i.at[s, zz], m["m1_r"].at[s, zz])
        value = p1[s, 0, zz] + m1i[s, zz]
        if zz > 0:
            value = value + z1i[s, zz]
        if zz < Z - 1:
            value = value + z1i[s, Z]
        p1[s, 0, zz] = value
        go(lambda: remote(p1.at[s, 0, zz], x1i.at[s], m["x1_s"].at[s], m["x1_r"].at[s], across))

    def x_step(kind, s, t, zz):
        v = order_static(zz)[t]
        if kind == "G":
            own_send(s, v, x, ACROSS, across)
        elif kind == "F":
            x_sum(s, v)
        else:
            x_near(s, zz)

    def x_arrival(s, t, zz):
        v = order_static(zz)[t]
        own_wait(s, v, x_other, core)
        own_send(s, v, x_other, MATE, mate)

    def events(step):
        for zz in range(Z):
            log[0] = by_z[zz]

            @pl.when(z == zz)
            def _():
                for direction in (UP, DOWN):
                    if in_direction(direction, zz) > 0 and 0 <= step - 1 < TOTAL:
                        z_arrival(direction, zz, step - 1)
                for direction in (UP, DOWN):
                    if in_direction(direction, zz) < Z - 1 and 2 <= step + 1 < TOTAL:
                        z_send(direction, zz, step + 1)
                if step in X_SENDS:
                    x_step(*X_SENDS[step], zz)
                if step in X_TAKES:
                    x_arrival(*X_TAKES[step], zz)

            log[0] = common

    def begin(s):
        own_send(s, z, x, ACROSS, across)
        own_send(s, z, x, MATE, mate)
        near_send(s, z, MATE - 1, mate)

    for zz in range(Z):
        log[0] = by_z[zz]

        @pl.when(z == zz)
        def _():
            for direction in (UP, DOWN):
                if in_direction(direction, zz) < Z - 1:
                    z_send(direction, zz, 0)

        log[0] = common
    own_send(0, z, x, ACROSS, across)
    own_send(0, z, x, MATE, mate)

    mask(near_tiles[0])
    near[0, z, core_rows(core), :] = fac[:, columns(near_tiles[0])]
    near_send(0, z, MATE - 1, mate)
    for zz in range(Z):
        log[0] = by_z[zz]

        @pl.when(z == zz)
        def _():
            for direction in (UP, DOWN):
                if in_direction(direction, zz) < Z - 1:
                    z_send(direction, zz, 1)

        log[0] = common

    for t in (sum_tiles[0], sum_tiles[1], near_tiles[1], own_tiles[1]):
        mask(t)
    for n, t in enumerate((sum_tiles[0], sum_tiles[1], near_tiles[0], near_tiles[1])):
        high, low = split(fac[:, columns(t)])
        lr_hi[:, columns(n)] = high
        lr_lo[:, columns(n)] = low

    def chip_job(q):
        v = order(3 - q // 2)
        other = q % 2 == 0
        side = 1 if other else 0
        chip = job_chip(q)
        load_anc(q).wait()

        def both(i, carry):
            c = core + (1 - 2 * core) * (1 - i)
            pair = split(a_buf[q % 4, core_rows(c), :])
            count = (4 if other else 2) * tile
            value = dot3(pair, (lr_hi[:, :count], lr_lo[:, :count]))
            for s in range(STAGES):
                p0[s, 1 - i, side, v] = value[:, columns(s)]
                if other:
                    p1[s, 1 - i, v] = value[:, columns(2 + s)]
            return carry

        lax.fori_loop(0, 2, both, 0)
        for s in range(STAGES):
            go(lambda s=s: remote(p0.at[s, 1, side, v], m0i.at[s, side, v], m["m0_s"].at[s, side, v], m["m0_r"].at[s, side, v], mate))
            if other:
                go(lambda s=s: remote(p1.at[s, 1, v], m1i.at[s, v], m["m1_s"].at[s, v], m["m1_r"].at[s, v], mate))

        def flip(c, carry):
            high, low = split(a_buf[q % 4, core_rows(c), :].T)
            at = pl.ds(pl.multiple_of(c * rows, rows), rows)
            tr_hi[chip, :, at] = high
            tr_lo[chip, :, at] = low
            return carry

        lax.fori_loop(0, 2, flip, 0)
        if q + 4 < 8:
            load_anc(q + 4).start()

    def pair_job(block, total, chip, first):
        high, low = split(block)
        left, rest = tr_hi[chip], tr_lo[chip]
        wide = jnp.dot(left, jnp.concatenate([high, low], axis=1), preferred_element_type=jnp.float32)
        value = wide[:, :tile] + (wide[:, tile:] + jnp.dot(rest, high, preferred_element_type=jnp.float32))
        if first:
            total[...] = value
        else:
            total[...] += value

    def own_job(s, t, other):
        zz = order(t)
        xx = 1 - x if other else x
        own_wait(s, zz, xx, 1 - core)
        pair_job(own[s, zz * 2 + xx], y_own.at[s], zz * 2 + xx, t == 0 and not other)

    def near_job(s, t):
        zz = order(t)
        near_wait(s, zz, 1 - core)
        pair_job(near[s, zz], y_near.at[s], zz * 2 + x, t == 0)

    def finish_own(s):
        cols_ref[:, columns(own_tiles[s])] = y_own[s]

    def finish(s):
        arrive(x1i.at[s], m["x1_r"].at[s])
        cols_ref[:, columns(near_tiles[s])] = y_near[s] + x1i[s]
        arrive(m0i.at[s, 0, z], m["m0_r"].at[s, 0, z])
        arrive(x0i.at[s, z], m["x0_r"].at[s, z])
        value = p0[s, 0, 0, z] + m0i[s, 0, z] + x0i[s, z]
        low = z0i[s, z]
        high = z0i[s, Z]
        value = value + jnp.where(z > 0, low, 0.0) + jnp.where(z < Z - 1, high, 0.0)
        cols_ref[:, columns(sum_tiles[s])] = value

    half_cols = 3 * tile
    sum_list = (
        [(q, p) for q in (3, 4, 5) for p in range(q + 1)],
        [(2, p) for p in range(3)],
        [(q, p) for q in (0, 1) for p in range(q + 1)],
    )

    def inner_early():
        flipped = split(cols_ref[:, half_cols:].T)
        value = dot3(flipped, split(fac[...]))
        for n, (q, p) in enumerate(sum_list[0]):
            m["part0"][n] = value[(q - 3) * tile : (q - 2) * tile, columns(p)]

    def inner_middle():
        value = dot3(split(cols_ref[:, columns(2)].T), split(fac[:, :half_cols]))
        for n, (q, p) in enumerate(sum_list[1]):
            m["part1"][n] = value[:, columns(p)]

    def inner_late():
        value = dot3((lt_hi[:width, :], lt_lo[:width, :]), split(cols_ref[:, :width]))
        for n, (q, p) in enumerate(sum_list[2]):
            m["part2"][n] = value[columns(q), columns(p)]

    groups = {
        "mate": (2, core, lambda n: index(z, x, n)),
        "x": (2, x, lambda n: index(z, n, core)),
        "z": (Z, z, lambda n: index(n, x, core)),
        "lane": (LANES, lane, lambda n: n * 2 + core),
    }

    def reducer(s):
        plan = LEVELS[s]
        sums = m[f"sum{s}"]
        sizes = [tile]
        for name in plan:
            sizes.append(sizes[-1] // groups[name][0])
        base = [0]
        for name, size in zip(plan, sizes[1:]):
            base.append(base[-1] + groups[name][1] * size)

        def held(level):
            return m[f"part{s}"] if level == 0 else m[f"held{s}_{level}"]

        def peer_of(level, d):
            count, mine, _ = groups[plan[level]]
            return 1 - mine if count == 2 else lax.rem(mine + d, count)

        def send_down(level):
            count, mine, device = groups[plan[level]]
            size = sizes[level + 1]
            for d in range(1, count):
                def make(d=d):
                    peer = peer_of(level, d)
                    src = held(level).at[:, pl.ds(pl.multiple_of(peer * size, size), size), :]
                    return remote(
                        src, m[f"slot{s}_{level}"].at[mine], m[f"ds{s}"].at[level, peer], m[f"dr{s}"].at[level, mine], device(peer)
                    )
                go(make)

        def take_down(level):
            count, mine, device = groups[plan[level]]
            size = sizes[level + 1]
            slot = m[f"slot{s}_{level}"]
            total = held(level)[:, pl.ds(pl.multiple_of(mine * size, size), size), :]
            for d in range(1, count):
                peer = peer_of(level, d)
                arrive(slot.at[peer], m[f"dr{s}"].at[level, peer])
                total = total + slot[peer]
            if level + 1 < len(plan):
                held(level + 1)[...] = total
            else:
                sums[:, pl.ds(pl.multiple_of(base[-1], size), size), :] = total

        def part_at(level, owner):
            size = sizes[level + 1]
            return sums.at[:, pl.ds(pl.multiple_of(base[level] + owner * size, size), size), :]

        def send_up(level):
            count, mine, device = groups[plan[level]]
            for d in range(1, count):
                def make(d=d):
                    peer = peer_of(level, d)
                    ref = part_at(level, mine)
                    return remote(ref, ref, m[f"us{s}"].at[level, peer], m[f"ur{s}"].at[level, mine], device(peer))
                go(make)

        def take_up(level):
            count, mine, device = groups[plan[level]]
            for d in range(1, count):
                peer = peer_of(level, d)
                arrive(part_at(level, peer), m[f"ur{s}"].at[level, peer])

        steps = [lambda: send_down(0)]
        for level in range(len(plan)):
            def step(level=level):
                take_down(level)
                if level + 1 < len(plan):
                    send_down(level + 1)
                else:
                    send_up(level)
            steps.append(step)
        for level in range(len(plan) - 1, -1, -1):
            def step(level=level):
                take_up(level)
                if level > 0:
                    send_up(level - 1)
            steps.append(step)
        return steps

    inner = m["inner"]
    blocks = [(2, 2), (2, 1), (2, 0), (1, 1), (1, 0), (0, 0)]

    def place(s):
        for n, (q, p) in enumerate(sum_list[s]):
            value = m[f"sum{s}"][n]
            at = blocks.index((q // 2, p // 2))
            inner[at, (q % 2) * tile : (q % 2 + 1) * tile, (p % 2) * tile : (p % 2 + 1) * tile] = value
            if q // 2 == p // 2 and q != p:
                inner[at, (p % 2) * tile : (p % 2 + 1) * tile, (q % 2) * tile : (q % 2 + 1) * tile] = value.T

    def n_block(j, k):
        return inner[blocks.index((j, k))]

    def fac_block(j, k):
        return win_st[win_pairs.index((j, k))]

    def save_block(j, k):
        block = out_ref.at[pl.ds(j * width, width), pl.ds(k * width, width)]
        target = out_hbm.at[pl.ds(j * width, width), pl.ds(k * width, width)]
        return pltpu.make_async_copy(block, target, m["save_sem"].at[j, k])

    def save_column(k):
        at = pl.ds(k * width, width)
        return pltpu.make_async_copy(cols_ref.at[:, at], cols_hbm.at[:, at], m["save_sem"].at[3, k])

    def put(j, k, value):
        out_ref[j * width : (j + 1) * width, k * width : (k + 1) * width] = value
        save_block(j, k).start()

    def got(j, k):
        return out_ref[j * width : (j + 1) * width, k * width : (k + 1) * width]

    early = m["early"]

    def window_first():
        put(2, 2, piv_st[2] + n_block(2, 2))
        value = n_block(2, 1) - mul(got(2, 2), fac_block(2, 1))
        put(2, 1, value)
        put(1, 2, value.T)
        value = n_block(2, 0) - mul(got(2, 1), fac_block(1, 0)) - mul(got(2, 2), fac_block(2, 0))
        put(2, 0, value)
        put(0, 2, value.T)

    def window_second():
        flip21 = split(fac_block(2, 1).T)
        known = piv_st[1] - mul(n_block(2, 1).T, fac_block(2, 1)) - dot3(flip21, split(got(2, 1)))
        early[0] = known
        turned = dot3(flip21, split(n_block(2, 0)))
        left = jnp.concatenate([fac_block(2, 1).T, known, got(1, 2)], axis=1)
        right = jnp.concatenate([n_block(2, 0), fac_block(1, 0), fac_block(2, 0)], axis=0)
        early[1] = mul(left, right)
        early[2] = (
            piv_st[0]
            + mul(turned.T, fac_block(1, 0))
            - mul(n_block(2, 0).T, fac_block(2, 0))
            - mul(fac_block(2, 0).T, got(2, 0))
        )

    def window_last():
        put(1, 1, early[0] + n_block(1, 1))
        value = n_block(1, 0) - early[1] - mul(n_block(1, 1), fac_block(1, 0))
        put(1, 0, value)
        put(0, 1, value.T)
        put(0, 0, early[2] + n_block(0, 0) - mul(n_block(1, 0).T, fac_block(1, 0)) - mul(fac_block(1, 0).T, value))

    def column(k):
        return cols_ref[:, k * width : (k + 1) * width]

    def put_column(k):
        value = column(k)
        for j in range(k + 1, 3):
            value = value + mul(column(j), fac_block(j, k))
        cols_ref[:, k * width : (k + 1) * width] = -value

    chip_job(0)
    chip_job(1)
    x_sum(0, order(3))
    load_piv.start()
    for n in range(3):
        load_win(n).start()
    events(1)
    chip_job(2)
    chip_job(3)
    events(2)
    chip_job(4)
    chip_job(5)
    own[1, lane, core_rows(core), :] = fac[:, columns(own_tiles[1])]
    near[1, z, core_rows(core), :] = fac[:, columns(near_tiles[1])]
    events(3)
    chip_job(6)
    chip_job(7)
    events(4)
    own_job(0, 0, False)
    own_job(0, 1, False)
    events(5)
    near_job(0, 0)
    near_job(0, 1)
    own_job(0, 0, True)
    own_job(0, 1, True)
    events(6)
    begin(1)
    own_job(0, 2, False)
    near_job(0, 2)
    own_job(0, 2, True)
    events(7)
    own_job(0, 3, False)
    high, low = split(fac[:, :half_cols].T)
    lt_hi[...] = high
    lt_lo[...] = low
    events(8)
    near_job(0, 3)
    events(9)
    own_job(0, 3, True)
    finish_own(0)
    finish(0)
    inner_early()
    cols_ref[:, 2 * width :] = -cols_ref[:, 2 * width :]
    save_column(2).start()
    first, middle, last = reducer(0), reducer(1), reducer(2)
    first[0]()
    events(10)
    own_job(1, 0, False)
    first[1]()
    events(11)
    own_job(1, 1, False)
    near_job(1, 0)
    near_job(1, 1)
    own_job(1, 0, True)
    events(12)
    first[2]()
    events(13)
    own_job(1, 1, True)
    own_job(1, 2, False)
    near_job(1, 2)
    events(14)
    first[3]()
    own_job(1, 2, True)
    load_piv.wait()
    for n in range(3):
        load_win(n).wait()
    events(15)
    own_job(1, 3, False)
    events(16)
    near_job(1, 3)
    own_job(1, 3, True)
    finish_own(1)
    inner_middle()
    middle[0]()
    middle[1]()
    events(17)
    finish(1)
    inner_late()
    last[0]()
    first[4]()
    middle[2]()
    put_column(1)
    save_column(1).start()
    last[1]()
    put_column(0)
    save_column(0).start()
    first[5]()
    middle[3]()
    last[2]()
    first[6]()
    place(0)
    window_first()
    middle[4]()
    window_second()
    for step in last[3:]:
        step()
    place(1)
    place(2)
    window_last()
    for k in range(3):
        save_column(k).wait()
        for j in range(3):
            save_block(j, k).wait()

    for make in common:
        make().wait_send()
    for zz in range(Z):

        @pl.when(z == zz)
        def _():
            for make in by_z[zz]:
                make().wait_send()


LEVELS = (("mate", "x", "z"), ("mate", "lane"), ("mate", "lane"))
COUNT = dict(mate=2, x=2, z=Z, lane=LANES)


def fused(anc_inverse, anc_factor, win_factor, pivot_inverse, structure):
    steps, width = pivot_inverse.shape[:2]
    rows, all_cols = anc_factor.shape
    tile = width // 2
    f32, b16 = jnp.float32, jnp.bfloat16
    dma = pltpu.SemaphoreType.DMA
    block = (rows, tile)
    pair = (2 * rows, tile)
    spaces = dict(
        cols=pltpu.VMEM((rows, all_cols), f32),
        out=pltpu.VMEM((all_cols, all_cols), f32),
        save_sem=dma((4, 3)),
        fac=pltpu.VMEM((rows, all_cols), f32),
        a_buf=pltpu.VMEM((4, 2 * rows, rows), f32),
        win=pltpu.VMEM((3, width, width), f32),
        piv=pltpu.VMEM(pivot_inverse.shape, f32),
        lr_hi=pltpu.VMEM((rows, 4 * tile), b16),
        lr_lo=pltpu.VMEM((rows, 4 * tile), b16),
        lt_hi=pltpu.VMEM((3 * tile, rows), b16),
        lt_lo=pltpu.VMEM((3 * tile, rows), b16),
        tr_hi=pltpu.VMEM((LANES, rows, 2 * rows), b16),
        tr_lo=pltpu.VMEM((LANES, rows, 2 * rows), b16),
        own=pltpu.VMEM((STAGES, LANES, *pair), f32),
        near=pltpu.VMEM((STAGES, Z, *pair), f32),
        y_own=pltpu.VMEM((STAGES, *block), f32),
        y_near=pltpu.VMEM((STAGES, *block), f32),
        p0=pltpu.VMEM((STAGES, 2, 2, Z, *block), f32),
        m0i=pltpu.VMEM((STAGES, 2, Z, *block), f32),
        x0i=pltpu.VMEM((STAGES, Z, *block), f32),
        z0i=pltpu.VMEM((STAGES, Z + 1, *block), f32),
        p1=pltpu.VMEM((STAGES, 2, Z, *block), f32),
        m1i=pltpu.VMEM((STAGES, Z, *block), f32),
        x1i=pltpu.VMEM((STAGES, *block), f32),
        z1i=pltpu.VMEM((STAGES, Z + 1, *block), f32),
        inner=pltpu.VMEM((6, width, width), f32),
        early=pltpu.VMEM((3, width, width), f32),
        load_sem=dma((13,)),
        own_s=dma((STAGES, 4, LANES)),
        own_r=dma((STAGES, LANES, 2)),
        near_s=dma((STAGES, 3, Z)),
        near_r=dma((STAGES, Z, 2)),
        m0_s=dma((STAGES, 2, Z)),
        m0_r=dma((STAGES, 2, Z)),
        x0_s=dma((STAGES, Z)),
        x0_r=dma((STAGES, Z)),
        z0_s=dma((STAGES, Z)),
        z0_r=dma((STAGES, Z + 1)),
        m1_s=dma((STAGES, Z)),
        m1_r=dma((STAGES, Z)),
        x1_s=dma((STAGES,)),
        x1_r=dma((STAGES,)),
        z1_s=dma((STAGES, Z)),
        z1_r=dma((STAGES, Z + 1)),
    )
    for s, plan in enumerate(LEVELS):
        tiles = (15, 3, 3)[s]
        size = tile
        spaces[f"part{s}"] = pltpu.VMEM((tiles, tile, tile), f32)
        spaces[f"sum{s}"] = pltpu.VMEM((tiles, tile, tile), f32)
        for level, name in enumerate(plan):
            size //= COUNT[name]
            spaces[f"slot{s}_{level}"] = pltpu.VMEM((COUNT[name], tiles, size, tile), f32)
            if level + 1 < len(plan):
                spaces[f"held{s}_{level + 1}"] = pltpu.VMEM((tiles, size, tile), f32)
        for kind in ("ds", "dr", "us", "ur"):
            spaces[f"{kind}{s}"] = dma((len(plan), LANES))
    whole = pl.BlockSpec(memory_space=pl.ANY)
    return pl.pallas_call(
        functools.partial(fused_kernel, tuple(spaces), width),
        out_shape=(
            jax.ShapeDtypeStruct((rows, all_cols), f32),
            jax.ShapeDtypeStruct((all_cols, all_cols), f32),
        ),
        in_specs=[whole, whole, whole, whole, pl.BlockSpec(memory_space=pltpu.SMEM)],
        out_specs=(whole, whole),
        scratch_shapes=list(spaces.values()),
        compiler_params=pltpu.CompilerParams(
            collective_id=0, has_side_effects=True, vmem_limit_bytes=63 * 2**20
        ),
    )(anc_inverse, anc_factor, win_factor, pivot_inverse, structure)


def land_kernel(parts, *refs):
    count = len(parts)
    sources, targets = refs[:count], refs[count : 2 * count]
    held, sem = refs[2 * count : 3 * count], refs[3 * count]
    copies = []
    for n, pieces in enumerate(parts):
        size = sources[n].shape[0] // pieces
        for i in range(pieces):
            at = pl.ds(i * size, size)
            read = pltpu.make_async_copy(sources[n].at[at, :], held[n].at[at, :], sem.at[0, len(copies)])
            write = pltpu.make_async_copy(held[n].at[at, :], targets[n].at[at, :], sem.at[1, len(copies)])
            read.start()
            copies.append((read, write))
    for read, write in copies:
        read.wait()
        write.start()
    for read, write in copies:
        write.wait()


def land(*arrays):
    whole = pl.BlockSpec(memory_space=pl.ANY)
    parts = (3, 6)
    return pl.pallas_call(
        functools.partial(land_kernel, parts),
        out_shape=tuple(jax.ShapeDtypeStruct(a.shape, a.dtype) for a in arrays),
        in_specs=[whole] * len(arrays),
        out_specs=(whole,) * len(arrays),
        scratch_shapes=[pltpu.VMEM(a.shape, a.dtype) for a in arrays] + [pltpu.SemaphoreType.DMA((2, sum(parts)))],
    )(*arrays)


precise = lax.Precision.HIGHEST


def product(left, right):
    return jnp.dot(left, right, precision=precise, preferred_element_type=jnp.float32)


def on_device(anc_inverse, anc_factor, win_factor, pivot_inverse, structure):
    row_count = lax.axis_size("prow")
    col_count = lax.axis_size("pcol")
    steps, width = pivot_inverse.shape[:2]
    fits = steps == 3 and 2 * anc_factor.shape[0] == 3 * width and width % 256 == 0
    if row_count == 1 and col_count == 4 * Z and fits:
        return land(*fused(anc_inverse, anc_factor, win_factor, pivot_inverse, structure))
    row_index = lax.axis_index("prow")
    col_index = lax.axis_index("pcol")
    block_rows = anc_inverse.shape[0]
    block_cols = anc_inverse.shape[1]
    steps_total = pivot_inverse.shape[0]
    width = pivot_inverse.shape[1]
    all_cols = anc_factor.shape[1]
    block_count = structure.shape[1]
    ratio_cols = col_count // row_count
    share_rows = block_rows // col_count
    structure_cols = structure.T.astype(jnp.float32)
    global_rows = col_index * block_cols + lax.iota(jnp.int32, block_cols)
    onehot_rows = (
        (global_rows // width)[:, None] == lax.iota(jnp.int32, block_count)[None, :]
    ).astype(jnp.float32)
    kept_rows = product(onehot_rows, structure_cols)
    share_offset = col_index * share_rows
    share_global = (row_index * col_count + col_index) * share_rows + lax.iota(
        jnp.int32, share_rows
    )
    onehot_share = (
        (share_global // width)[:, None] == lax.iota(jnp.int32, block_count)[None, :]
    ).astype(jnp.float32)
    kept_share = product(onehot_share, structure_cols)
    slot_ids = lax.iota(jnp.int32, col_count)
    source_flag = (slot_ids // row_count == col_index - row_index * ratio_cols).astype(jnp.float32)
    pieces = jnp.tile(anc_factor.reshape(row_count, share_rows, all_cols), (ratio_cols, 1, 1))
    outgoing = pieces * source_flag[:, None, None]
    incoming = lax.all_to_all(outgoing, "pcol", split_axis=0, concat_axis=0, tiled=True)
    factor_share = jnp.sum(incoming, axis=0)
    column_store = {}
    share_store = {}
    window_blocks = {}
    for k in range(steps_total - 1, -1, -1):
        first_col = k * width
        factor_now = anc_factor[:, first_col : first_col + width] * kept_rows[:, k : k + 1]
        share_factor = factor_share[:, first_col : first_col + width] * kept_share[:, k : k + 1]
        finished = list(range(k + 1, steps_total))
        if finished:
            stacked = jnp.concatenate([column_store[j] for j in finished], axis=1)
            factor_win = win_factor[first_col + width :, first_col : first_col + width]

        def term_rows(start, count, factor_now=factor_now):
            return product(anc_inverse, factor_now)

        share_image = lax.psum_scatter(
            term_rows(jnp.int32(0), share_rows * lax.axis_size("pcol")),
            "pcol",
            scatter_dimension=0,
            tiled=True,
        )
        if finished:
            share_image = share_image + product(
                lax.dynamic_slice_in_dim(stacked, share_offset, share_rows, 0), factor_win
            )
        share_column = -share_image
        column_now = lax.all_gather(share_column, "pcol", axis=0, tiled=True)
        crossings = [product(share_store[j].T, share_factor) for j in finished]
        pivot_part = product(share_factor.T, share_column)
        cross_sums = []
        if finished:
            cross_total = lax.psum(jnp.stack(crossings), ("prow", "pcol"))
            cross_sums = [cross_total[position] for position in range(len(finished))]
        pivot_sum = lax.psum(pivot_part, ("prow", "pcol"))
        for position, j in enumerate(finished):
            running = cross_sums[position]
            for i in finished:
                running = running + product(
                    window_blocks[j, i],
                    win_factor[i * width : (i + 1) * width, first_col : first_col + width],
                )
            window_blocks[j, k] = -running
            window_blocks[k, j] = -running.T
        pivot_block = pivot_inverse[k] - pivot_sum
        for j in finished:
            pivot_block = pivot_block - product(
                win_factor[j * width : (j + 1) * width, first_col : first_col + width].T,
                window_blocks[j, k],
            )
        window_blocks[k, k] = pivot_block
        column_store[k] = column_now
        share_store[k] = share_column
    anc_columns = jnp.concatenate([share_store[k] for k in range(steps_total)], axis=1)
    win_inverse = jnp.concatenate(
        [
            jnp.concatenate([window_blocks[i, k] for k in range(steps_total)], axis=1)
            for i in range(steps_total)
        ],
        axis=0,
    )
    return (anc_columns, win_inverse)


def solution(mesh):
    in_specs = (
        P(("pole", "prow"), "pcol"),
        P(("pole", "pcol"), None),
        P("pole", None),
        P("pole", None, None),
        P(),
    )
    out_specs = (P(("pole", "prow", "pcol"), None), P("pole", None))
    return jax.shard_map(
        on_device, mesh=mesh, in_specs=in_specs, out_specs=out_specs, check_vma=False
    )
```

```python
import functools

import jax
import jax.numpy as jnp
from jax import lax
from jax.experimental import pallas as pl
from jax.experimental.pallas import tpu as pltpu
from jax.sharding import PartitionSpec as P

MESH = pl.DeviceIdType.MESH
UP, DOWN, ACROSS, MATE = range(4)
Z = 4
LANES = 8


def split(value):
    high = value.astype(jnp.bfloat16)
    low = (value - high.astype(jnp.float32)).astype(jnp.bfloat16)
    return high, low


def dot3(left, right):
    (lh, ll), (rh, rl) = left, right
    dot = functools.partial(jnp.dot, preferred_element_type=jnp.float32)
    return dot(lh, rh) + (dot(lh, rl) + dot(ll, rh))


def mul(left, right):
    return dot3(split(left), split(right))


STAGES = 2
FIRST = (0, 8)
TOTAL = 16


def item_list(s, u):
    if u == 0:
        rest = [("R1", 3), ("R0", 3), ("R1", 2), ("R0", 2), ("R1", 1), ("R0", 1)]
        return [("G", 0), ("H", 0)] + rest
    far = []
    if u == 1:
        rest = [("R1", 3)] + far + [("R0", 3), ("R1", 2), ("R0", 2)]
        return [("G", 1), ("H", 1), ("G", 0), ("H", 0)] + rest
    rest = [("G", 1), ("H", 1), ("G", 0), ("H", 0), ("R1", 3)] + far + [("R0", 3)]
    return [("G", 2), ("H", 2)] + rest


def item_at(u, n):
    s = 1 if n >= FIRST[1] else 0
    items = item_list(s, u)
    n -= FIRST[s]
    return (s, *items[n]) if n < len(items) else (s, "", 0)


X_SENDS = {
    1: ("G", 0, 1), 2: ("F", 0, 2), 3: ("G", 0, 2), 4: ("F", 0, 1), 5: ("G", 0, 3), 6: ("F", 0, 0), 7: ("R", 0, 0), 8: ("F", 1, 3),
    9: ("F", 1, 2), 10: ("G", 1, 1), 11: ("F", 1, 1), 12: ("G", 1, 2), 13: ("F", 1, 0), 14: ("G", 1, 3), 15: ("R", 1, 0),
}
X_TAKES = {2: (0, 0), 3: (0, 1), 5: (0, 2), 7: (0, 3), 9: (1, 0), 12: (1, 1), 14: (1, 2), 16: (1, 3)}


def order_static(z):
    return ([0, 1, 2, 3], [1, 0, 2, 3], [2, 3, 1, 0], [3, 2, 1, 0])[z]


def fused_kernel(names, width, anc_ref, fac_ref, win_ref, piv_ref, str_ref, cols_hbm, out_hbm, *scratch):
    m = dict(zip(names, scratch, strict=True))
    cols_ref, out_ref = m["cols"], m["out"]
    fac, a_buf, win_st, piv_st = m["fac"], m["a_buf"], m["win"], m["piv"]
    lr_hi, lr_lo, lt_hi, lt_lo = m["lr_hi"], m["lr_lo"], m["lt_hi"], m["lt_lo"]
    tr_hi, tr_lo = m["tr_hi"], m["tr_lo"]
    own, near, y_own, y_near = m["own"], m["near"], m["y_own"], m["y_near"]
    p0, m0i, x0i, z0i = m["p0"], m["m0i"], m["x0i"], m["z0i"]
    p1, m1i, x1i, z1i = m["p1"], m["m1i"], m["x1i"], m["z1i"]

    me = lax.axis_index("pcol")
    core = lax.rem(me, 2)
    x = lax.rem(me // 2, 2)
    z = me // 4
    lane = me // 2
    rows = fac.shape[0]
    tile = width // 2
    mate = me + 1 - 2 * core

    def index(zz, xx, cc):
        return (zz * 2 + xx) * 2 + cc

    x_other = 1 - x
    across = index(z, x_other, core)

    def order(t):
        inner = (0, 0, 2, 3) if t else (1, 1, 1, 1)
        lowmid = inner[t] if t else 1
        highmid = 3 - lowmid
        return jnp.where(z == 0, t, jnp.where(z == 1, lowmid, jnp.where(z == 2, highmid, 3 - t)))

    def job_chip(q):
        return order(3 - q // 2) * 2 + (1 - x if q % 2 == 0 else x)

    def load_anc(q):
        at = pl.ds(pl.multiple_of(job_chip(q) * 2 * rows, 2 * rows), 2 * rows)
        return pltpu.make_async_copy(anc_ref.at[at, :], a_buf.at[q % 4], m["load_sem"].at[q])

    lead = pl.ds(5 * tile, tile)
    load_lead = pltpu.make_async_copy(fac_ref.at[:, lead], fac.at[:, lead], m["load_sem"].at[8])
    rest = pl.ds(0, 5 * tile)
    load_fac = pltpu.make_async_copy(fac_ref.at[:, rest], fac.at[:, rest], m["load_sem"].at[13])
    load_piv = pltpu.make_async_copy(piv_ref, piv_st, m["load_sem"].at[9])
    win_pairs = [(2, 1), (1, 0), (2, 0)]

    def load_win(n):
        j, k = win_pairs[n]
        block = win_ref.at[pl.ds(j * width, width), pl.ds(k * width, width)]
        return pltpu.make_async_copy(block, win_st.at[n], m["load_sem"].at[10 + n])

    load_lead.start()
    load_fac.start()
    for q in range(4):
        load_anc(q).start()

    barrier = pltpu.get_barrier_semaphore()
    for d in range(1, LANES):
        peer = lax.rem(lane + d, LANES) * 2 + core
        pl.semaphore_signal(barrier, inc=1, device_id={"pcol": peer}, device_id_type=MESH)
    pl.semaphore_signal(barrier, inc=1, device_id={"pcol": mate}, device_id_type=MESH)

    common = []
    by_z = [[] for _ in range(Z)]
    log = [common]

    def go(make):
        make().start()
        log[0].append(make)

    def remote(src, dst, ssem, rsem, dest):
        return pltpu.make_async_remote_copy(
            src_ref=src, dst_ref=dst, send_sem=ssem, recv_sem=rsem, device_id={"pcol": dest}, device_id_type=MESH
        )

    def arrive(dst, rsem):
        remote(dst, dst, rsem, rsem, mate).wait_recv()

    def core_rows(c):
        return pl.ds(pl.multiple_of(c * rows, rows), rows)

    def own_at(s, zz, xx, c):
        return own.at[s, zz * 2 + xx, core_rows(c), :]

    def near_at(s, zz, c):
        return near.at[s, zz, core_rows(c), :]

    def own_send(s, zz, xx, kind, dest):
        def make():
            ref = own_at(s, zz, xx, core)
            return remote(ref, ref, m["own_s"].at[s, kind, zz * 2 + xx], m["own_r"].at[s, zz * 2 + xx, core], dest)
        go(make)

    def near_send(s, zz, kind, dest):
        def make():
            ref = near_at(s, zz, core)
            return remote(ref, ref, m["near_s"].at[s, kind, zz], m["near_r"].at[s, zz, core], dest)
        go(make)

    def own_wait(s, zz, xx, c):
        arrive(own_at(s, zz, xx, c), m["own_r"].at[s, zz * 2 + xx, c])

    def near_wait(s, zz, c):
        arrive(near_at(s, zz, c), m["near_r"].at[s, zz, c])

    def columns(t):
        return slice(t * tile, (t + 1) * tile)

    def mask(t):
        for piece in range(rows // tile):
            block = (me * (rows // tile) + piece) // 2
            kept = str_ref[t // 2, block].astype(jnp.float32)
            at = slice(piece * tile, (piece + 1) * tile)
            fac[at, columns(t)] = fac[at, columns(t)] * kept

    own_tiles, near_tiles, sum_tiles = (5, 2), (4, 1), (3, 0)

    load_lead.wait()
    mask(own_tiles[0])
    own[0, lane, core_rows(core), :] = fac[:, columns(own_tiles[0])]
    pl.semaphore_wait(barrier, LANES)

    def in_direction(direction, zz):
        return zz if direction == UP else Z - 1 - zz

    z_dests = (me + 4, me - 4)

    def z_dest(direction):
        return z_dests[direction]

    def landing(direction, zz, dest_z):
        return Z if direction == DOWN and dest_z == zz else dest_z

    def z_send(direction, zz, n):
        s, kind, v = item_at(in_direction(direction, zz), n)
        vz = in_direction(direction, v)
        first = in_direction(direction, zz) == 0
        dest = z_dest(direction)
        there = zz + 1 if direction == UP else zz - 1
        if kind == "G":
            own_send(s, vz, x, direction, dest)
        elif kind == "H":
            near_send(s, vz, direction, dest)
        elif kind == "X":
            own_send(s, vz, x_other, direction, dest)
        elif kind == "R1":
            arrive(m1i.at[s, vz], m["m1_r"].at[s, vz])
            value = p1[s, 0, vz] + m1i[s, vz]
            if not first:
                value = value + z1i[s, vz]
            p1[s, 0, vz] = value
            at = landing(direction, there, vz)
            go(lambda: remote(p1.at[s, 0, vz], z1i.at[s, at], m["z1_s"].at[s, vz], m["z1_r"].at[s, at], z_dest(direction)))
        elif kind == "R0":
            arrive(m0i.at[s, 0, vz], m["m0_r"].at[s, 0, vz])
            arrive(x0i.at[s, vz], m["x0_r"].at[s, vz])
            value = p0[s, 0, 0, vz] + m0i[s, 0, vz] + x0i[s, vz]
            if not first:
                value = value + z0i[s, vz]
            p0[s, 0, 0, vz] = value
            at = landing(direction, there, vz)
            go(lambda: remote(p0.at[s, 0, 0, vz], z0i.at[s, at], m["z0_s"].at[s, vz], m["z0_r"].at[s, at], z_dest(direction)))

    def z_arrival(direction, zz, n):
        u = in_direction(direction, zz)
        s, kind, v = item_at(u - 1, n)
        vz = in_direction(direction, v)
        if kind == "G":
            own_wait(s, vz, x, core)
            own_send(s, vz, x, MATE, mate)
        elif kind == "H":
            near_wait(s, vz, core)
            near_send(s, vz, MATE - 1, mate)
        elif kind == "X":
            own_wait(s, vz, x_other, core)
            own_send(s, vz, x_other, MATE, mate)
        elif kind == "R1":
            at = landing(direction, zz, vz)
            arrive(z1i.at[s, at], m["z1_r"].at[s, at])
        elif kind == "R0":
            at = landing(direction, zz, vz)
            arrive(z0i.at[s, at], m["z0_r"].at[s, at])

    def x_sum(s, v):
        arrive(m0i.at[s, 1, v], m["m0_r"].at[s, 1, v])
        p0[s, 0, 1, v] = p0[s, 0, 1, v] + m0i[s, 1, v]
        go(lambda: remote(p0.at[s, 0, 1, v], x0i.at[s, v], m["x0_s"].at[s, v], m["x0_r"].at[s, v], across))

    def x_near(s, zz):
        arrive(m1i.at[s, zz], m["m1_r"].at[s, zz])
        value = p1[s, 0, zz] + m1i[s, zz]
        if zz > 0:
            value = value + z1i[s, zz]
        if zz < Z - 1:
            value = value + z1i[s, Z]
        p1[s, 0, zz] = value
        go(lambda: remote(p1.at[s, 0, zz], x1i.at[s], m["x1_s"].at[s], m["x1_r"].at[s], across))

    def x_step(kind, s, t, zz):
        v = order_static(zz)[t]
        if kind == "G":
            own_send(s, v, x, ACROSS, across)
        elif kind == "F":
            x_sum(s, v)
        else:
            x_near(s, zz)

    def x_arrival(s, t, zz):
        v = order_static(zz)[t]
        own_wait(s, v, x_other, core)
        own_send(s, v, x_other, MATE, mate)

    def events(step):
        for zz in range(Z):
            log[0] = by_z[zz]

            @pl.when(z == zz)
            def _():
                for direction in (UP, DOWN):
                    if in_direction(direction, zz) > 0 and 0 <= step - 1 < TOTAL:
                        z_arrival(direction, zz, step - 1)
                for direction in (UP, DOWN):
                    if in_direction(direction, zz) < Z - 1 and 2 <= step + 1 < TOTAL:
                        z_send(direction, zz, step + 1)
                if step in X_SENDS:
                    x_step(*X_SENDS[step], zz)
                if step in X_TAKES:
                    x_arrival(*X_TAKES[step], zz)

            log[0] = common

    def begin(s):
        own_send(s, z, x, ACROSS, across)
        own_send(s, z, x, MATE, mate)
        near_send(s, z, MATE - 1, mate)

    for zz in range(Z):
        log[0] = by_z[zz]

        @pl.when(z == zz)
        def _():
            for direction in (UP, DOWN):
                if in_direction(direction, zz) < Z - 1:
                    z_send(direction, zz, 0)

        log[0] = common
    own_send(0, z, x, ACROSS, across)
    own_send(0, z, x, MATE, mate)

    load_fac.wait()
    mask(near_tiles[0])
    near[0, z, core_rows(core), :] = fac[:, columns(near_tiles[0])]
    near_send(0, z, MATE - 1, mate)
    for zz in range(Z):
        log[0] = by_z[zz]

        @pl.when(z == zz)
        def _():
            for direction in (UP, DOWN):
                if in_direction(direction, zz) < Z - 1:
                    z_send(direction, zz, 1)

        log[0] = common

    for t in (sum_tiles[0], sum_tiles[1], near_tiles[1], own_tiles[1]):
        mask(t)
    for n, t in enumerate((sum_tiles[0], sum_tiles[1], near_tiles[0], near_tiles[1])):
        high, low = split(fac[:, columns(t)])
        lr_hi[:, columns(n)] = high
        lr_lo[:, columns(n)] = low

    def chip_job(q):
        v = order(3 - q // 2)
        other = q % 2 == 0
        side = 1 if other else 0
        chip = job_chip(q)
        load_anc(q).wait()

        def both(i, carry):
            c = core + (1 - 2 * core) * (1 - i)
            pair = split(a_buf[q % 4, core_rows(c), :])
            count = (4 if other else 2) * tile
            value = dot3(pair, (lr_hi[:, :count], lr_lo[:, :count]))
            for s in range(STAGES):
                p0[s, 1 - i, side, v] = value[:, columns(s)]
                if other:
                    p1[s, 1 - i, v] = value[:, columns(2 + s)]
            return carry

        lax.fori_loop(0, 2, both, 0)
        for s in range(STAGES):
            go(lambda s=s: remote(p0.at[s, 1, side, v], m0i.at[s, side, v], m["m0_s"].at[s, side, v], m["m0_r"].at[s, side, v], mate))
            if other:
                go(lambda s=s: remote(p1.at[s, 1, v], m1i.at[s, v], m["m1_s"].at[s, v], m["m1_r"].at[s, v], mate))

        def flip(c, carry):
            high, low = split(a_buf[q % 4, core_rows(c), :].T)
            at = pl.ds(pl.multiple_of(c * rows, rows), rows)
            tr_hi[chip, :, at] = high
            tr_lo[chip, :, at] = low
            return carry

        lax.fori_loop(0, 2, flip, 0)
        if q + 4 < 8:
            load_anc(q + 4).start()

    def pair_job(block, total, chip, first):
        high, low = split(block)
        left, rest = tr_hi[chip], tr_lo[chip]
        wide = jnp.dot(left, jnp.concatenate([high, low], axis=1), preferred_element_type=jnp.float32)
        value = wide[:, :tile] + (wide[:, tile:] + jnp.dot(rest, high, preferred_element_type=jnp.float32))
        if first:
            total[...] = value
        else:
            total[...] += value

    def own_job(s, t, other):
        zz = order(t)
        xx = 1 - x if other else x
        own_wait(s, zz, xx, 1 - core)
        pair_job(own[s, zz * 2 + xx], y_own.at[s], zz * 2 + xx, t == 0 and not other)

    def near_job(s, t):
        zz = order(t)
        near_wait(s, zz, 1 - core)
        pair_job(near[s, zz], y_near.at[s], zz * 2 + x, t == 0)

    def finish_own(s):
        cols_ref[:, columns(own_tiles[s])] = y_own[s]

    def finish(s):
        arrive(x1i.at[s], m["x1_r"].at[s])
        cols_ref[:, columns(near_tiles[s])] = y_near[s] + x1i[s]
        arrive(m0i.at[s, 0, z], m["m0_r"].at[s, 0, z])
        arrive(x0i.at[s, z], m["x0_r"].at[s, z])
        value = p0[s, 0, 0, z] + m0i[s, 0, z] + x0i[s, z]
        low = z0i[s, z]
        high = z0i[s, Z]
        value = value + jnp.where(z > 0, low, 0.0) + jnp.where(z < Z - 1, high, 0.0)
        cols_ref[:, columns(sum_tiles[s])] = value

    half_cols = 3 * tile
    sum_list = (
        [(q, p) for q in (3, 4, 5) for p in range(q + 1)],
        [(2, p) for p in range(3)],
        [(q, p) for q in (0, 1) for p in range(q + 1)],
    )

    def inner_early():
        flipped = split(cols_ref[:, half_cols:].T)
        value = dot3(flipped, split(fac[...]))
        for n, (q, p) in enumerate(sum_list[0]):
            m["part0"][n] = value[(q - 3) * tile : (q - 2) * tile, columns(p)]

    def inner_middle():
        value = dot3(split(cols_ref[:, columns(2)].T), split(fac[:, :half_cols]))
        for n, (q, p) in enumerate(sum_list[1]):
            m["part1"][n] = value[:, columns(p)]

    def inner_late():
        value = dot3((lt_hi[:width, :], lt_lo[:width, :]), split(cols_ref[:, :width]))
        for n, (q, p) in enumerate(sum_list[2]):
            m["part2"][n] = value[columns(q), columns(p)]

    groups = {
        "mate": (2, core, lambda n: index(z, x, n)),
        "x": (2, x, lambda n: index(z, n, core)),
        "z": (Z, z, lambda n: index(n, x, core)),
        "lane": (LANES, lane, lambda n: n * 2 + core),
    }

    def reducer(s):
        plan = LEVELS[s]
        sums = m[f"sum{s}"]
        sizes = [tile]
        for name in plan:
            sizes.append(sizes[-1] // groups[name][0])
        base = [0]
        for name, size in zip(plan, sizes[1:]):
            base.append(base[-1] + groups[name][1] * size)

        def held(level):
            return m[f"part{s}"] if level == 0 else m[f"held{s}_{level}"]

        def peer_of(level, d):
            count, mine, _ = groups[plan[level]]
            return 1 - mine if count == 2 else lax.rem(mine + d, count)

        def send_down(level):
            count, mine, device = groups[plan[level]]
            size = sizes[level + 1]
            for d in range(1, count):
                def make(d=d):
                    peer = peer_of(level, d)
                    src = held(level).at[:, pl.ds(pl.multiple_of(peer * size, size), size), :]
                    return remote(
                        src, m[f"slot{s}_{level}"].at[mine], m[f"ds{s}"].at[level, peer], m[f"dr{s}"].at[level, mine], device(peer)
                    )
                go(make)

        def take_down(level):
            count, mine, device = groups[plan[level]]
            size = sizes[level + 1]
            slot = m[f"slot{s}_{level}"]
            total = held(level)[:, pl.ds(pl.multiple_of(mine * size, size), size), :]
            for d in range(1, count):
                peer = peer_of(level, d)
                arrive(slot.at[peer], m[f"dr{s}"].at[level, peer])
                total = total + slot[peer]
            if level + 1 < len(plan):
                held(level + 1)[...] = total
            else:
                sums[:, pl.ds(pl.multiple_of(base[-1], size), size), :] = total

        def part_at(level, owner):
            size = sizes[level + 1]
            return sums.at[:, pl.ds(pl.multiple_of(base[level] + owner * size, size), size), :]

        def send_up(level):
            count, mine, device = groups[plan[level]]
            for d in range(1, count):
                def make(d=d):
                    peer = peer_of(level, d)
                    ref = part_at(level, mine)
                    return remote(ref, ref, m[f"us{s}"].at[level, peer], m[f"ur{s}"].at[level, mine], device(peer))
                go(make)

        def take_up(level):
            count, mine, device = groups[plan[level]]
            for d in range(1, count):
                peer = peer_of(level, d)
                arrive(part_at(level, peer), m[f"ur{s}"].at[level, peer])

        steps = [lambda: send_down(0)]
        for level in range(len(plan)):
            def step(level=level):
                take_down(level)
                if level + 1 < len(plan):
                    send_down(level + 1)
                else:
                    send_up(level)
            steps.append(step)
        for level in range(len(plan) - 1, -1, -1):
            def step(level=level):
                take_up(level)
                if level > 0:
                    send_up(level - 1)
            steps.append(step)
        return steps

    inner = m["inner"]
    blocks = [(2, 2), (2, 1), (2, 0), (1, 1), (1, 0), (0, 0)]

    def place(s):
        for n, (q, p) in enumerate(sum_list[s]):
            value = m[f"sum{s}"][n]
            at = blocks.index((q // 2, p // 2))
            inner[at, (q % 2) * tile : (q % 2 + 1) * tile, (p % 2) * tile : (p % 2 + 1) * tile] = value
            if q // 2 == p // 2 and q != p:
                inner[at, (p % 2) * tile : (p % 2 + 1) * tile, (q % 2) * tile : (q % 2 + 1) * tile] = value.T

    def n_block(j, k):
        return inner[blocks.index((j, k))]

    def fac_block(j, k):
        return win_st[win_pairs.index((j, k))]

    def save_block(j, k):
        block = out_ref.at[pl.ds(j * width, width), pl.ds(k * width, width)]
        target = out_hbm.at[pl.ds(j * width, width), pl.ds(k * width, width)]
        return pltpu.make_async_copy(block, target, m["save_sem"].at[j, k])

    def save_column(k):
        at = pl.ds(k * width, width)
        return pltpu.make_async_copy(cols_ref.at[:, at], cols_hbm.at[:, at], m["save_sem"].at[3, k])

    def put(j, k, value):
        out_ref[j * width : (j + 1) * width, k * width : (k + 1) * width] = value
        save_block(j, k).start()

    def got(j, k):
        return out_ref[j * width : (j + 1) * width, k * width : (k + 1) * width]

    early = m["early"]

    def window_first():
        put(2, 2, piv_st[2] + n_block(2, 2))
        value = n_block(2, 1) - mul(got(2, 2), fac_block(2, 1))
        put(2, 1, value)
        put(1, 2, value.T)
        value = n_block(2, 0) - mul(got(2, 1), fac_block(1, 0)) - mul(got(2, 2), fac_block(2, 0))
        put(2, 0, value)
        put(0, 2, value.T)

    def window_second():
        flip21 = split(fac_block(2, 1).T)
        known = piv_st[1] - mul(n_block(2, 1).T, fac_block(2, 1)) - dot3(flip21, split(got(2, 1)))
        early[0] = known
        turned = dot3(flip21, split(n_block(2, 0)))
        left = jnp.concatenate([fac_block(2, 1).T, known, got(1, 2)], axis=1)
        right = jnp.concatenate([n_block(2, 0), fac_block(1, 0), fac_block(2, 0)], axis=0)
        early[1] = mul(left, right)
        early[2] = (
            piv_st[0]
            + mul(turned.T, fac_block(1, 0))
            - mul(n_block(2, 0).T, fac_block(2, 0))
            - mul(fac_block(2, 0).T, got(2, 0))
        )

    def window_last():
        put(1, 1, early[0] + n_block(1, 1))
        value = n_block(1, 0) - early[1] - mul(n_block(1, 1), fac_block(1, 0))
        put(1, 0, value)
        put(0, 1, value.T)
        put(0, 0, early[2] + n_block(0, 0) - mul(n_block(1, 0).T, fac_block(1, 0)) - mul(fac_block(1, 0).T, value))

    def column(k):
        return cols_ref[:, k * width : (k + 1) * width]

    def put_column(k):
        value = column(k)
        for j in range(k + 1, 3):
            value = value + mul(column(j), fac_block(j, k))
        cols_ref[:, k * width : (k + 1) * width] = -value

    chip_job(0)
    chip_job(1)
    x_sum(0, order(3))
    load_piv.start()
    for n in range(3):
        load_win(n).start()
    events(1)
    chip_job(2)
    chip_job(3)
    events(2)
    chip_job(4)
    chip_job(5)
    own[1, lane, core_rows(core), :] = fac[:, columns(own_tiles[1])]
    near[1, z, core_rows(core), :] = fac[:, columns(near_tiles[1])]
    events(3)
    chip_job(6)
    chip_job(7)
    events(4)
    own_job(0, 0, False)
    own_job(0, 1, False)
    events(5)
    near_job(0, 0)
    near_job(0, 1)
    own_job(0, 0, True)
    own_job(0, 1, True)
    events(6)
    begin(1)
    own_job(0, 2, False)
    near_job(0, 2)
    own_job(0, 2, True)
    events(7)
    own_job(0, 3, False)
    high, low = split(fac[:, :half_cols].T)
    lt_hi[...] = high
    lt_lo[...] = low
    events(8)
    near_job(0, 3)
    events(9)
    own_job(0, 3, True)
    finish_own(0)
    finish(0)
    inner_early()
    cols_ref[:, 2 * width :] = -cols_ref[:, 2 * width :]
    save_column(2).start()
    first, middle, last = reducer(0), reducer(1), reducer(2)
    first[0]()
    events(10)
    own_job(1, 0, False)
    first[1]()
    events(11)
    own_job(1, 1, False)
    near_job(1, 0)
    near_job(1, 1)
    own_job(1, 0, True)
    events(12)
    first[2]()
    events(13)
    own_job(1, 1, True)
    own_job(1, 2, False)
    near_job(1, 2)
    events(14)
    first[3]()
    own_job(1, 2, True)
    load_piv.wait()
    for n in range(3):
        load_win(n).wait()
    events(15)
    own_job(1, 3, False)
    events(16)
    near_job(1, 3)
    own_job(1, 3, True)
    finish_own(1)
    inner_middle()
    middle[0]()
    middle[1]()
    events(17)
    finish(1)
    inner_late()
    last[0]()
    first[4]()
    middle[2]()
    put_column(1)
    save_column(1).start()
    last[1]()
    put_column(0)
    save_column(0).start()
    first[5]()
    middle[3]()
    last[2]()
    first[6]()
    place(0)
    window_first()
    middle[4]()
    window_second()
    for step in last[3:]:
        step()
    place(1)
    place(2)
    window_last()
    for k in range(3):
        save_column(k).wait()
        for j in range(3):
            save_block(j, k).wait()

    for make in common:
        make().wait_send()
    for zz in range(Z):

        @pl.when(z == zz)
        def _():
            for make in by_z[zz]:
                make().wait_send()


LEVELS = (("mate", "x", "z"), ("mate", "lane"), ("mate", "lane"))
COUNT = dict(mate=2, x=2, z=Z, lane=LANES)


def fused(anc_inverse, anc_factor, win_factor, pivot_inverse, structure):
    steps, width = pivot_inverse.shape[:2]
    rows, all_cols = anc_factor.shape
    tile = width // 2
    f32, b16 = jnp.float32, jnp.bfloat16
    dma = pltpu.SemaphoreType.DMA
    block = (rows, tile)
    pair = (2 * rows, tile)
    spaces = dict(
        cols=pltpu.VMEM((rows, all_cols), f32),
        out=pltpu.VMEM((all_cols, all_cols), f32),
        save_sem=dma((4, 3)),
        fac=pltpu.VMEM((rows, all_cols), f32),
        a_buf=pltpu.VMEM((4, 2 * rows, rows), f32),
        win=pltpu.VMEM((3, width, width), f32),
        piv=pltpu.VMEM(pivot_inverse.shape, f32),
        lr_hi=pltpu.VMEM((rows, 4 * tile), b16),
        lr_lo=pltpu.VMEM((rows, 4 * tile), b16),
        lt_hi=pltpu.VMEM((3 * tile, rows), b16),
        lt_lo=pltpu.VMEM((3 * tile, rows), b16),
        tr_hi=pltpu.VMEM((LANES, rows, 2 * rows), b16),
        tr_lo=pltpu.VMEM((LANES, rows, 2 * rows), b16),
        own=pltpu.VMEM((STAGES, LANES, *pair), f32),
        near=pltpu.VMEM((STAGES, Z, *pair), f32),
        y_own=pltpu.VMEM((STAGES, *block), f32),
        y_near=pltpu.VMEM((STAGES, *block), f32),
        p0=pltpu.VMEM((STAGES, 2, 2, Z, *block), f32),
        m0i=pltpu.VMEM((STAGES, 2, Z, *block), f32),
        x0i=pltpu.VMEM((STAGES, Z, *block), f32),
        z0i=pltpu.VMEM((STAGES, Z + 1, *block), f32),
        p1=pltpu.VMEM((STAGES, 2, Z, *block), f32),
        m1i=pltpu.VMEM((STAGES, Z, *block), f32),
        x1i=pltpu.VMEM((STAGES, *block), f32),
        z1i=pltpu.VMEM((STAGES, Z + 1, *block), f32),
        inner=pltpu.VMEM((6, width, width), f32),
        early=pltpu.VMEM((3, width, width), f32),
        load_sem=dma((14,)),
        own_s=dma((STAGES, 4, LANES)),
        own_r=dma((STAGES, LANES, 2)),
        near_s=dma((STAGES, 3, Z)),
        near_r=dma((STAGES, Z, 2)),
        m0_s=dma((STAGES, 2, Z)),
        m0_r=dma((STAGES, 2, Z)),
        x0_s=dma((STAGES, Z)),
        x0_r=dma((STAGES, Z)),
        z0_s=dma((STAGES, Z)),
        z0_r=dma((STAGES, Z + 1)),
        m1_s=dma((STAGES, Z)),
        m1_r=dma((STAGES, Z)),
        x1_s=dma((STAGES,)),
        x1_r=dma((STAGES,)),
        z1_s=dma((STAGES, Z)),
        z1_r=dma((STAGES, Z + 1)),
    )
    for s, plan in enumerate(LEVELS):
        tiles = (15, 3, 3)[s]
        size = tile
        spaces[f"part{s}"] = pltpu.VMEM((tiles, tile, tile), f32)
        spaces[f"sum{s}"] = pltpu.VMEM((tiles, tile, tile), f32)
        for level, name in enumerate(plan):
            size //= COUNT[name]
            spaces[f"slot{s}_{level}"] = pltpu.VMEM((COUNT[name], tiles, size, tile), f32)
            if level + 1 < len(plan):
                spaces[f"held{s}_{level + 1}"] = pltpu.VMEM((tiles, size, tile), f32)
        for kind in ("ds", "dr", "us", "ur"):
            spaces[f"{kind}{s}"] = dma((len(plan), LANES))
    whole = pl.BlockSpec(memory_space=pl.ANY)
    return pl.pallas_call(
        functools.partial(fused_kernel, tuple(spaces), width),
        out_shape=(
            jax.ShapeDtypeStruct((rows, all_cols), f32),
            jax.ShapeDtypeStruct((all_cols, all_cols), f32),
        ),
        in_specs=[whole, whole, whole, whole, pl.BlockSpec(memory_space=pltpu.SMEM)],
        out_specs=(whole, whole),
        scratch_shapes=list(spaces.values()),
        compiler_params=pltpu.CompilerParams(
            collective_id=0, has_side_effects=True, vmem_limit_bytes=63 * 2**20
        ),
    )(anc_inverse, anc_factor, win_factor, pivot_inverse, structure)


def land_kernel(parts, *refs):
    count = len(parts)
    sources, targets = refs[:count], refs[count : 2 * count]
    held, sem = refs[2 * count : 3 * count], refs[3 * count]
    copies = []
    for n, pieces in enumerate(parts):
        size = sources[n].shape[0] // pieces
        for i in range(pieces):
            at = pl.ds(i * size, size)
            read = pltpu.make_async_copy(sources[n].at[at, :], held[n].at[at, :], sem.at[0, len(copies)])
            write = pltpu.make_async_copy(held[n].at[at, :], targets[n].at[at, :], sem.at[1, len(copies)])
            read.start()
            copies.append((read, write))
    for read, write in copies:
        read.wait()
        write.start()
    for read, write in copies:
        write.wait()


def land(*arrays):
    whole = pl.BlockSpec(memory_space=pl.ANY)
    parts = (3, 6)
    return pl.pallas_call(
        functools.partial(land_kernel, parts),
        out_shape=tuple(jax.ShapeDtypeStruct(a.shape, a.dtype) for a in arrays),
        in_specs=[whole] * len(arrays),
        out_specs=(whole,) * len(arrays),
        scratch_shapes=[pltpu.VMEM(a.shape, a.dtype) for a in arrays] + [pltpu.SemaphoreType.DMA((2, sum(parts)))],
    )(*arrays)


precise = lax.Precision.HIGHEST


def product(left, right):
    return jnp.dot(left, right, precision=precise, preferred_element_type=jnp.float32)


def on_device(anc_inverse, anc_factor, win_factor, pivot_inverse, structure):
    row_count = lax.axis_size("prow")
    col_count = lax.axis_size("pcol")
    steps, width = pivot_inverse.shape[:2]
    fits = steps == 3 and 2 * anc_factor.shape[0] == 3 * width and width % 256 == 0
    if row_count == 1 and col_count == 4 * Z and fits:
        return land(*fused(anc_inverse, anc_factor, win_factor, pivot_inverse, structure))
    row_index = lax.axis_index("prow")
    col_index = lax.axis_index("pcol")
    block_rows = anc_inverse.shape[0]
    block_cols = anc_inverse.shape[1]
    steps_total = pivot_inverse.shape[0]
    width = pivot_inverse.shape[1]
    all_cols = anc_factor.shape[1]
    block_count = structure.shape[1]
    ratio_cols = col_count // row_count
    share_rows = block_rows // col_count
    structure_cols = structure.T.astype(jnp.float32)
    global_rows = col_index * block_cols + lax.iota(jnp.int32, block_cols)
    onehot_rows = (
        (global_rows // width)[:, None] == lax.iota(jnp.int32, block_count)[None, :]
    ).astype(jnp.float32)
    kept_rows = product(onehot_rows, structure_cols)
    share_offset = col_index * share_rows
    share_global = (row_index * col_count + col_index) * share_rows + lax.iota(
        jnp.int32, share_rows
    )
    onehot_share = (
        (share_global // width)[:, None] == lax.iota(jnp.int32, block_count)[None, :]
    ).astype(jnp.float32)
    kept_share = product(onehot_share, structure_cols)
    slot_ids = lax.iota(jnp.int32, col_count)
    source_flag = (slot_ids // row_count == col_index - row_index * ratio_cols).astype(jnp.float32)
    pieces = jnp.tile(anc_factor.reshape(row_count, share_rows, all_cols), (ratio_cols, 1, 1))
    outgoing = pieces * source_flag[:, None, None]
    incoming = lax.all_to_all(outgoing, "pcol", split_axis=0, concat_axis=0, tiled=True)
    factor_share = jnp.sum(incoming, axis=0)
    column_store = {}
    share_store = {}
    window_blocks = {}
    for k in range(steps_total - 1, -1, -1):
        first_col = k * width
        factor_now = anc_factor[:, first_col : first_col + width] * kept_rows[:, k : k + 1]
        share_factor = factor_share[:, first_col : first_col + width] * kept_share[:, k : k + 1]
        finished = list(range(k + 1, steps_total))
        if finished:
            stacked = jnp.concatenate([column_store[j] for j in finished], axis=1)
            factor_win = win_factor[first_col + width :, first_col : first_col + width]

        def term_rows(start, count, factor_now=factor_now):
            return product(anc_inverse, factor_now)

        share_image = lax.psum_scatter(
            term_rows(jnp.int32(0), share_rows * lax.axis_size("pcol")),
            "pcol",
            scatter_dimension=0,
            tiled=True,
        )
        if finished:
            share_image = share_image + product(
                lax.dynamic_slice_in_dim(stacked, share_offset, share_rows, 0), factor_win
            )
        share_column = -share_image
        column_now = lax.all_gather(share_column, "pcol", axis=0, tiled=True)
        crossings = [product(share_store[j].T, share_factor) for j in finished]
        pivot_part = product(share_factor.T, share_column)
        cross_sums = []
        if finished:
            cross_total = lax.psum(jnp.stack(crossings), ("prow", "pcol"))
            cross_sums = [cross_total[position] for position in range(len(finished))]
        pivot_sum = lax.psum(pivot_part, ("prow", "pcol"))
        for position, j in enumerate(finished):
            running = cross_sums[position]
            for i in finished:
                running = running + product(
                    window_blocks[j, i],
                    win_factor[i * width : (i + 1) * width, first_col : first_col + width],
                )
            window_blocks[j, k] = -running
            window_blocks[k, j] = -running.T
        pivot_block = pivot_inverse[k] - pivot_sum
        for j in finished:
            pivot_block = pivot_block - product(
                win_factor[j * width : (j + 1) * width, first_col : first_col + width].T,
                window_blocks[j, k],
            )
        window_blocks[k, k] = pivot_block
        column_store[k] = column_now
        share_store[k] = share_column
    anc_columns = jnp.concatenate([share_store[k] for k in range(steps_total)], axis=1)
    win_inverse = jnp.concatenate(
        [
            jnp.concatenate([window_blocks[i, k] for k in range(steps_total)], axis=1)
            for i in range(steps_total)
        ],
        axis=0,
    )
    return (anc_columns, win_inverse)


def solution(mesh):
    in_specs = (
        P(("pole", "prow"), "pcol"),
        P(("pole", "pcol"), None),
        P("pole", None),
        P("pole", None, None),
        P(),
    )
    out_specs = (P(("pole", "prow", "pcol"), None), P("pole", None))
    return jax.shard_map(
        on_device, mesh=mesh, in_specs=in_specs, out_specs=out_specs, check_vma=False
    )
```
